32 devices in a mesh: gx: 2 (over x), gy: 4 (over z), scene: 4 (over y, core).
Axes of the slice: x: 2, y: 2, z: 4, core: 2. Of those that a mesh axis runs over, the one named last changes fastest.
Arguments:
- field_in: bfloat16 [4, 32, 32, 64, 256], P('scene', None, 'gx', 'gy'), may hold values from -6 to 6
- grad_pre: bfloat16 [4, 32, 32, 64, 256], P('scene', None, 'gx', 'gy'), may hold values from -6 to 6
- spec_weight: bfloat16 [24, 24, 13, 2, 1024], P('gx', 'gy'), may hold values from -6 to 6
- point_weight: bfloat16 [32, 32], replicated, may hold values from -1 to 1
Outputs:
- grad_field: bfloat16 [4, 32, 32, 64, 256], P('scene', None, 'gx', 'gy')
- grad_spec: float32 [24, 24, 13, 2, 1024], P('gx', 'gy', None, None, 'scene')
The draws below stay inside these ranges and needn't reach their ends.
All inputs are finite; a program needn't handle non-finite values.
Results may differ from the reference program's by a relative error of at most 0.0045.
Values may be sent and summed in bfloat16 or wider, within the bound.
No kernel may reach another device: no remote copies, remote signals or barrier semaphores. Data moves between devices by JAX's collectives and lax.ppermute only.
A program may use at most 128 MiB of HBM per device.

```python
import math
import jax
import jax.numpy as jnp
from jax import lax

C = 32
MX = 24
MY = 24
MZ = 13
NZ = 256
SCENES = 4
NX = 32
NY = 64


def block_scale(own_key, dims, cuts, least, largest):
    def one(dim, parts):
        steps = jax.random.uniform(jax.random.fold_in(jax.random.fold_in(own_key, 6), dim), (parts,), jnp.float32, least / len(cuts), largest / len(cuts))
        return jnp.repeat(jnp.exp(steps), dims[dim] // parts).reshape((-1,) + (1,) * (len(dims) - dim - 1))

    level = one(*cuts[0])
    for cut in cuts[1:]:
        level = level * one(*cut)
    return level


def normal_values(own_key, extent, spread, most, pieces=(), kind=jnp.bfloat16):
    result = spread * jax.random.normal(own_key, extent, jnp.float32)
    if pieces:
        result = result * block_scale(own_key, extent, pieces, -0.22, 0.18)
    return jnp.clip(result, -most, most).astype(kind)


def setup_inputs(seed: int = 0) -> dict:
    seeds = jax.random.split(jax.random.key(seed), 5)
    field_in = normal_values(seeds[0], (SCENES, C, NX, NY, NZ), 1.0, 6.0, ((0, 4), (2, 2), (3, 4)))
    grad_pre = normal_values(seeds[1], (SCENES, C, NX, NY, NZ), 1.0, 6.0, ((0, 4), (2, 2), (3, 4)))
    spec_weight = normal_values(seeds[2], (MX, MY, MZ, 2, C * C), ((NX * NY * NZ / (4 * MX * MY * MZ * C)) ** 0.5), 6.0, ((0, 2), (1, 4)))
    point_weight = normal_values(seeds[3], (C, C), C ** -0.5, 1.0)
    return {"field_in": field_in, "grad_pre": grad_pre, "spec_weight": spec_weight, "point_weight": point_weight}


def angle_table(index, modes, positions, length):
    signed_freq = jnp.where(index < modes // 2, index, index - modes)
    turns = jnp.mod(signed_freq[..., None] * positions, length)
    return turns.astype(jnp.float32) * (2.0 * math.pi / length)


def forward_rotation(angles):
    cosine = jnp.cos(angles)
    sine = jnp.sin(angles)
    return jnp.stack([jnp.stack([cosine, sine], -1), jnp.stack([-sine, cosine], -1)], 0)


def inverse_rotation(angles):
    cosine = jnp.cos(angles)
    sine = jnp.sin(angles)
    return jnp.stack([jnp.stack([cosine, -sine], -1), jnp.stack([sine, cosine], -1)], 0)


def z_tables(modes_z, length):
    angles = angle_table(jnp.arange(modes_z, dtype=jnp.int32), 2 * modes_z, jnp.arange(length, dtype=jnp.int32), length)
    cosine = jnp.cos(angles)
    sine = jnp.sin(angles)
    forward_z = jnp.concatenate([cosine, -sine], 0).T.astype(jnp.bfloat16)
    inverse_z = jnp.stack([cosine, -sine], 0)
    return forward_z, inverse_z


def reference(field_in, grad_pre, spec_weight, point_weight):
    highest = lax.Precision.HIGHEST
    norm = float(NX * NY * NZ) ** -0.5
    forward_z, inverse_z = z_tables(MZ, NZ)
    angles_y = angle_table(jnp.arange(MY, dtype=jnp.int32), MY, jnp.arange(NY, dtype=jnp.int32), NY)
    angles_x = angle_table(jnp.arange(MX, dtype=jnp.int32), MX, jnp.arange(NX, dtype=jnp.int32), NX)
    forward_y = forward_rotation(angles_y)
    forward_x = forward_rotation(angles_x)
    inverse_y = inverse_rotation(angles_y)
    inverse_x = inverse_rotation(angles_x)
    z_weight = jnp.where(jnp.arange(MZ, dtype=jnp.int32) == 0, 1.0, 2.0).astype(jnp.float32)
    weights = spec_weight.astype(jnp.float32).reshape(MX, MY, MZ, 2, C, C)
    weight_re = weights[:, :, :, 0]
    weight_im = weights[:, :, :, 1]
    mixing = point_weight.astype(jnp.float32)
    grad_total = jnp.zeros((MX, MY, MZ, 2, C, C), jnp.float32)
    results = []
    for scene_index in range(SCENES):
        field_z = jnp.dot(field_in[scene_index].reshape(-1, NZ), forward_z, preferred_element_type=jnp.float32).reshape(C, NX, NY, 2, MZ)
        pre_z = jnp.dot(grad_pre[scene_index].reshape(-1, NZ), forward_z, preferred_element_type=jnp.float32).reshape(C, NX, NY, 2, MZ)
        along_z = jnp.stack([field_z, pre_z], 0)
        along_y = jnp.einsum('wcxypk,qjyp->wcxqjk', along_z, forward_y, precision=highest)
        spectra = jnp.einsum('wcxqjk,rixq->ijwcrk', along_y, forward_x, precision=highest) * norm
        field_hat = spectra[:, :, 0]
        grad_out = spectra[:, :, 1] * z_weight
        hat_re = field_hat[:, :, :, 0]
        hat_im = field_hat[:, :, :, 1]
        out_re = grad_out[:, :, :, 0]
        out_im = grad_out[:, :, :, 1]
        mode_re = jnp.einsum('abkio,abok->abik', weight_re, out_re, precision=highest) + jnp.einsum('abkio,abok->abik', weight_im, out_im, precision=highest)
        mode_im = jnp.einsum('abkio,abok->abik', weight_re, out_im, precision=highest) - jnp.einsum('abkio,abok->abik', weight_im, out_re, precision=highest)
        mode_grad = jnp.stack([mode_re, mode_im], 3)
        rounded = lax.optimization_barrier(mode_grad.astype(jnp.bfloat16)).astype(jnp.float32)
        grad_re = jnp.einsum('abok,abik->abkio', out_re, hat_re, precision=highest) + jnp.einsum('abok,abik->abkio', out_im, hat_im, precision=highest)
        grad_im = jnp.einsum('abok,abik->abkio', out_im, hat_re, precision=highest) - jnp.einsum('abok,abik->abkio', out_re, hat_im, precision=highest)
        grad_total = grad_total + jnp.stack([grad_re, grad_im], 3)
        back_y = jnp.einsum('ijcpk,qjyp->iycqk', rounded, inverse_y, precision=highest)
        back_modes = jnp.einsum('iycqk,rixq->xycrk', back_y, inverse_x, precision=highest)
        spectral_grad = jnp.einsum('xycrk,rkz->cxyz', back_modes, inverse_z, precision=highest) * norm
        local_grad = jnp.einsum('oi,oxyz->ixyz', mixing, grad_pre[scene_index].astype(jnp.float32))
        results.append((spectral_grad + local_grad).astype(jnp.bfloat16))
    return jnp.stack(results, 0), grad_total.reshape(MX, MY, MZ, 2, C * C)
```

```python
import functools
import math

import jax
import jax.numpy as jnp
import ml_dtypes
import numpy as np
from jax import lax
from jax.experimental import pallas as pl
from jax.experimental.pallas import tpu as pltpu
from jax.sharding import PartitionSpec as P

MX = 24
MY = 24
MZ = 13
LANES = 128
SPLIT = False
NT = (((1,), (1,)), ((), ()))
BF16 = ml_dtypes.bfloat16


def angles(xp, index, modes, positions, length):
    freq = xp.where(index < modes // 2, index, index - modes)
    turns = (freq[..., None] * positions) % length
    return turns.astype(np.float32) * np.float32(2.0 * math.pi / length)


def mode_angles(xp, rows, sizes, local_x, local_y):
    groups, groups_y, modes_xd, modes_yd, total_x, total_y = sizes
    owner = xp.repeat(xp.arange(groups, dtype=np.int32), rows)
    within = xp.tile(xp.arange(rows, dtype=np.int32), groups)
    kx = owner // groups_y * modes_xd + xp.minimum(within // modes_yd, modes_xd - 1)
    ky = owner % groups_y * modes_yd + within % modes_yd
    angle_x = angles(xp, kx, MX, local_x, total_x)
    angle_y = angles(xp, ky, MY, local_y, total_y)
    theta = (angle_x[:, :, None] + angle_y[:, None, :]).reshape(owner.shape[0], -1)
    return theta, (within < modes_xd * modes_yd)[:, None]


def split16(values):
    high = values.astype(BF16)
    low = (values - high.astype(np.float32)).astype(BF16)
    return high, low


def device_cells(xp, me, groups_y, cells_x, cells_y):
    local_x = me // groups_y * cells_x + xp.arange(cells_x, dtype=np.int32)
    local_y = me % groups_y * cells_y + xp.arange(cells_y, dtype=np.int32)
    return local_x, local_y


def forward_table(xp, first, rows, sizes, cells_x, cells_y):
    groups_y = sizes[1]
    parts = []
    for t in range(4):
        device = first + quad_offset(t, groups_y)
        theta, real = mode_angles(
            xp, rows, sizes, *device_cells(xp, device, groups_y, cells_x, cells_y)
        )
        both = xp.concatenate([xp.cos(theta), xp.sin(theta)], 1)
        parts.append(xp.stack(split16(xp.where(real, both, np.float32(0)))))
    return xp.stack(parts)


def inverse_table(xp, me, rows, sizes, cells_x, cells_y):
    theta, real = mode_angles(
        xp, rows, sizes, *device_cells(xp, me, sizes[1], cells_x, cells_y)
    )
    cosine = xp.where(real, xp.cos(theta), np.float32(0))
    sine = xp.where(real, xp.sin(theta), np.float32(0))
    return xp.concatenate([cosine.T, sine.T], 0).astype(BF16)


def quad_offset(t, groups_y):
    return t // 2 * groups_y + t % 2


def quad_of(r, groups_y):
    return r // groups_y % 2 * 2 + r % groups_y % 2


def z_angles(length):
    return angles(np, np.arange(MZ, dtype=np.int32), 2 * MZ, np.arange(length, dtype=np.int32), length)


def forward_z_table(length, block, kz_pad):
    theta = z_angles(length)
    parts = np.stack([np.cos(theta), -np.sin(theta)], 1)
    table = np.zeros((block, kz_pad, 2, block, length), np.float32)
    for c in range(block):
        table[c, :MZ, :, c] = parts
    return table.reshape(block, kz_pad * 2 * block, length).astype(BF16)


def inverse_z_table(length, per_tile, slot, norm):
    theta = z_angles(length)
    parts = np.stack([np.cos(theta), -np.sin(theta)], 0) * np.float32(norm)
    table = np.zeros((per_tile, 2, slot, per_tile, length), np.float32)
    for c in range(per_tile):
        table[c, :, :MZ, c] = parts
    high, low = split16(table.reshape(LANES, per_tile * length))
    return np.concatenate([high, low], 0)


def order_table(channels, kz_pad, per_tile, slot):
    table = np.zeros((kz_pad, 2, channels, channels // per_tile, per_tile, 2, slot), np.float32)
    for kz in range(MZ):
        for part in range(2):
            for c in range(channels):
                table[kz, part, c, c // per_tile, c % per_tile, part, kz] = 1
    return table.reshape(kz_pad * 2 * channels, -1).astype(BF16)


def spread_table(channels, half, copies):
    table = np.zeros((half, 2, channels, half, 2, copies.shape[0]), np.float32)
    for h in range(half):
        for part in range(2):
            table[h, part, copies, h, part, np.arange(copies.shape[0])] = 1
    return table.reshape(half * 2 * channels, -1).astype(BF16)


def gather_table(channels, copies):
    table = np.zeros((channels, channels, copies, channels), np.float32)
    for i in range(channels):
        table[i, :, :, i] = 1
    return table.reshape(channels * channels, -1).astype(BF16)


def cell_tables(channels, per_tile, cells_y):
    rows = np.zeros((per_tile, channels // per_tile, cells_y, channels), np.float32)
    for c in range(channels):
        rows[c % per_tile, c // per_tile, :, c] = 1
    columns = np.repeat(np.eye(channels, dtype=np.float32), cells_y, 1)
    return rows.reshape(-1, channels).astype(BF16), columns.astype(BF16)


def full(shape):
    return pl.BlockSpec(shape, lambda *_: (0,) * len(shape))


def params(mib):
    return pltpu.CompilerParams(vmem_limit_bytes=mib * 1024 * 1024)


def along_z_kernel(count, block, kz_pad, channels, info_ref, *refs):
    fields, z_ref = refs[:count], refs[count]
    outs, held = refs[count + 1 : count + 5], refs[count + 5]
    step = pl.program_id(0)
    for w, x_ref in enumerate(fields):
        total = None
        for c in range(block):
            term = lax.dot_general(z_ref[c], x_ref[c], NT, preferred_element_type=jnp.float32)
            total = term if total is None else total + term
        for k in range(2 * kz_pad):
            here = pl.multiple_of(k * channels + step * block, 8)
            held[w, pl.ds(here, block)] = total[k * block : (k + 1) * block]

    @pl.when(step == pl.num_programs(0) - 1)
    def _():
        for t in range(4):
            span = outs[t].shape[1]
            here = pl.multiple_of(jnp.bitwise_xor(info_ref[1], t) * span, 16)
            for w in range(count):
                outs[t][w] = held[w, pl.ds(here, span)].astype(jnp.bfloat16)


def along_z(info, fields, z_table, kz_pad, block):
    channels, cells, length = fields[0].shape
    count = len(fields)
    span = kz_pad * 2 * channels // 4
    chunk = jax.ShapeDtypeStruct((count, span, cells), jnp.bfloat16)
    return pl.pallas_call(
        functools.partial(along_z_kernel, count, block, kz_pad, channels),
        out_shape=[chunk] * 4,
        grid_spec=pltpu.PrefetchScalarGridSpec(
            num_scalar_prefetch=1,
            grid=(channels // block,),
            in_specs=[pl.BlockSpec((block, cells, length), lambda i, info: (i, 0, 0))] * count
            + [full(z_table.shape)],
            out_specs=[full(chunk.shape)] * 4,
            scratch_shapes=[pltpu.VMEM((count, kz_pad * 2 * channels, cells), jnp.float32)],
        ),
        compiler_params=params(12 * count),
        cost_estimate=pl.CostEstimate(
            flops=4 * count * cells * length * kz_pad * channels * block,
            bytes_accessed=2 * count * fields[0].size,
            transcendentals=0,
        ),
        name="along_z",
    )(info, *fields, z_table)


def plane_kernel(groups, rows, channels, info_ref, t_ref, *refs):
    sources, outs, (data, sums) = refs[:4], refs[4 : 4 + groups], refs[4 + groups :]
    count, span, cells = sources[0].shape
    step = pl.program_id(0)

    @pl.when(step == 0)
    def _():
        for t in range(4):
            place = jnp.bitwise_xor(info_ref[1], t)
            for w in range(count):
                value = sources[t][w]
                turned = []
                for k in range(0, span, 2 * channels):
                    turned += [value[k + channels : k + 2 * channels], -value[k : k + channels]]
                data[place, w * span : (w + 1) * span, :cells] = value
                data[place, w * span : (w + 1) * span, cells:] = jnp.concatenate(turned, 0)

    here = data[step]
    term = lax.dot_general(t_ref[0, 0, 0], here, NT, preferred_element_type=jnp.float32)
    term += lax.dot_general(t_ref[0, 0, 1], here, NT, preferred_element_type=jnp.float32)

    @pl.when(step == 0)
    def _():
        sums[...] = term

    @pl.when(step > 0)
    def _():
        sums[...] += term

    @pl.when(step == pl.num_programs(0) - 1)
    def _():
        for r in range(groups):
            own = pl.ds(pl.multiple_of(jnp.bitwise_xor(info_ref[0], r) * rows, 8), rows)
            for w in range(count):
                for j in range(span // LANES):
                    lane = w * span + j * LANES
                    outs[r][w, j] = sums[own, lane : lane + LANES].astype(jnp.bfloat16)


def plane(info, sources, table, groups, rows, channels):
    count, span, cells = sources[0].shape
    chunk = jax.ShapeDtypeStruct((count, span // LANES, rows, LANES), jnp.bfloat16)
    return pl.pallas_call(
        functools.partial(plane_kernel, groups, rows, channels),
        out_shape=[chunk] * groups,
        grid_spec=pltpu.PrefetchScalarGridSpec(
            num_scalar_prefetch=1,
            grid=(4,),
            in_specs=[
                pl.BlockSpec((1, 1) + table.shape[2:], lambda i, info: (info[2], i, 0, 0, 0))
            ]
            + [full(s.shape) for s in sources],
            out_specs=[full(chunk.shape)] * groups,
            scratch_shapes=[
                pltpu.VMEM((4, count * span, 2 * cells), jnp.bfloat16),
                pltpu.VMEM((groups * rows, count * span), jnp.float32),
            ],
        ),
        compiler_params=params(14 * count),
        cost_estimate=pl.CostEstimate(
            flops=32 * cells * count * span * groups * rows,
            bytes_accessed=2 * table[0].size,
            transcendentals=0,
        ),
        name="plane",
    )(info, table, *sources)


def add_sources(chunks, w, tile, mine, groups_y, held):
    per_quad = chunks[0].shape[1]
    for t in range(4):

        @pl.when(tile // per_quad == jnp.bitwise_xor(mine, t))
        def _(t=t):
            refs = [c for r, c in enumerate(chunks) if quad_of(r, groups_y) == t]
            total = refs[0][w, tile % per_quad].astype(jnp.float32)
            for ref in refs[1:]:
                total = total + ref[w, tile % per_quad].astype(jnp.float32)
            held[...] = total


def total_kernel(groups, groups_y, w, info_ref, *refs):
    scale_ref, out_ref, held = refs[groups:]
    add_sources(refs[:groups], w, pl.program_id(0), info_ref[1], groups_y, held)
    out_ref[0] = (held[...] * scale_ref[0]).astype(jnp.bfloat16)


def total(info, chunks, w, scale, groups_y):
    _, _, rows, _ = chunks[0].shape
    tiles = scale.shape[0]
    return pl.pallas_call(
        functools.partial(total_kernel, len(chunks), groups_y, w),
        out_shape=jax.ShapeDtypeStruct((tiles, rows, LANES), jnp.bfloat16),
        grid_spec=pltpu.PrefetchScalarGridSpec(
            num_scalar_prefetch=1,
            grid=(tiles,),
            in_specs=[full(c.shape) for c in chunks]
            + [pl.BlockSpec((1, 1, LANES), lambda i, info: (i, 0, 0))],
            out_specs=pl.BlockSpec((1, rows, LANES), lambda i, info: (i, 0, 0)),
            scratch_shapes=[pltpu.VMEM((rows, LANES), jnp.float32)],
        ),
        compiler_params=params(8),
        name="total",
    )(info, *chunks, scale)


def mix_kernel(groups, groups_y, w, info_ref, *refs):
    scale_ref, low_ref, high_ref, spread_ref, gather_ref, sum_ref, out_ref, held = refs[groups:]
    add_sources(refs[:groups], w, pl.program_id(0), info_ref[1], groups_y, held)
    values = (held[...] * scale_ref[0]).astype(jnp.bfloat16)
    sum_ref[0] = values
    rows = values.shape[0]
    wide = jnp.dot(values, spread_ref[...], preferred_element_type=jnp.float32)
    products = []
    for h, w_ref in enumerate((low_ref, high_ref)):
        out_re = wide[:, (2 * h) * LANES : (2 * h + 1) * LANES]
        out_im = wide[:, (2 * h + 1) * LANES : (2 * h + 2) * LANES]
        real, imag = [], []
        for k in range(w_ref.shape[3] // LANES):
            lane = slice(k * LANES, (k + 1) * LANES)
            w_re = w_ref[0, 0, :, lane].astype(jnp.float32)
            w_im = w_ref[0, 1, :, lane].astype(jnp.float32)
            real.append(w_re * out_re + w_im * out_im)
            imag.append(w_re * out_im - w_im * out_re)
        products += [jnp.concatenate(real, 1), jnp.concatenate(imag, 1)]
    sums = jnp.dot(
        jnp.concatenate(products, 0).astype(jnp.bfloat16),
        gather_ref[...],
        preferred_element_type=jnp.float32,
    )
    count = len(products)
    which = lax.broadcasted_iota(jnp.int32, (rows, LANES), 1) // (LANES // count)
    out = sums[:rows]
    for k in range(1, count):
        out = jnp.where(which == k, sums[k * rows : (k + 1) * rows], out)
    out_ref[0] = out.astype(jnp.bfloat16)


def mix(info, chunks, w, scale, weight, spread, gather, groups_y):
    _, _, rows, _ = chunks[0].shape
    tiles = scale.shape[0]
    last = weight.shape[0] - 1
    w_block = (1,) + weight.shape[1:]
    tile = pl.BlockSpec((1, rows, LANES), lambda i, info: (i, 0, 0))
    shape = jax.ShapeDtypeStruct((tiles, rows, LANES), jnp.bfloat16)
    return pl.pallas_call(
        functools.partial(mix_kernel, len(chunks), groups_y, w),
        out_shape=[shape, shape],
        grid_spec=pltpu.PrefetchScalarGridSpec(
            num_scalar_prefetch=1,
            grid=(tiles,),
            in_specs=[full(c.shape) for c in chunks]
            + [
                pl.BlockSpec((1, 1, LANES), lambda i, info: (i, 0, 0)),
                pl.BlockSpec(w_block, lambda i, info: (2 * i, 0, 0, 0)),
                pl.BlockSpec(w_block, lambda i, info: (jnp.minimum(2 * i + 1, last), 0, 0, 0)),
                full(spread.shape),
                full(gather.shape),
            ],
            out_specs=[tile, tile],
            scratch_shapes=[pltpu.VMEM((rows, LANES), jnp.float32)],
        ),
        compiler_params=params(16),
        cost_estimate=pl.CostEstimate(
            flops=8 * tiles * rows * gather.size, bytes_accessed=2 * weight.size, transcendentals=0
        ),
        name="mix",
    )(info, *chunks, scale, weight, weight, spread, gather)


def outer_kernel(scenes, info_ref, *refs):
    spectra, (spread_ref, pick_ref, out_ref) = refs[:scenes], refs[scenes:]
    rows, wide = out_ref.shape[2:]
    fields = jnp.dot(
        jnp.concatenate([ref[0, 0] for ref in spectra], 0),
        pick_ref[0],
        preferred_element_type=jnp.float32,
    )
    grads = jnp.dot(
        jnp.concatenate([ref[1, 0] for ref in spectra], 0),
        spread_ref[...],
        preferred_element_type=jnp.float32,
    )
    for h in range(out_ref.shape[0]):
        for k in range(wide // LANES):
            real, imag = 0.0, 0.0
            for s in range(scenes):
                here = slice(s * rows, (s + 1) * rows)
                lane = 2 * h * wide + k * LANES
                hat_re = fields[here, lane : lane + LANES]
                hat_im = fields[here, lane + wide : lane + wide + LANES]
                out_re = grads[here, 2 * h * LANES : (2 * h + 1) * LANES]
                out_im = grads[here, (2 * h + 1) * LANES : (2 * h + 2) * LANES]
                real += out_re * hat_re + out_im * hat_im
                imag += out_im * hat_re - out_re * hat_im
            out_ref[h, 0, :, k * LANES : (k + 1) * LANES] = real
            out_ref[h, 1, :, k * LANES : (k + 1) * LANES] = imag


def outer(info, spectra, spread, pick):
    _, tiles, rows, _ = spectra[0].shape
    wide = pick.shape[2] // 4
    block = pl.BlockSpec((2, 1, rows, LANES), lambda i, info: (0, i, 0, 0))
    return pl.pallas_call(
        functools.partial(outer_kernel, len(spectra)),
        out_shape=jax.ShapeDtypeStruct((2 * tiles, 2, rows, wide), jnp.float32),
        grid_spec=pltpu.PrefetchScalarGridSpec(
            num_scalar_prefetch=1,
            grid=(tiles,),
            in_specs=[block] * len(spectra)
            + [
                full(spread.shape),
                pl.BlockSpec((1,) + pick.shape[1:], lambda i, info: (info[4], 0, 0)),
            ],
            out_specs=pl.BlockSpec((2, 2, rows, wide), lambda i, info: (i, 0, 0, 0)),
        ),
        compiler_params=params(16),
        cost_estimate=pl.CostEstimate(
            flops=2 * tiles * rows * 4 * LANES * 12 * LANES,
            bytes_accessed=16 * tiles * rows * wide + 8 * tiles * rows * LANES * len(spectra),
            transcendentals=0,
        ),
        name="outer",
    )(info, *spectra, spread, pick)


def inverse_kernel(groups, per_tile, info_ref, *refs):
    chunks = refs[:groups]
    t_ref, order_ref, z_ref, point_ref, row_ref, column_ref, grad_ref = refs[groups : groups + 7]
    out_ref, modes, held, mixing = refs[groups + 7 :]
    channels, here, cells_y, length = grad_ref.shape
    rows = chunks[0].shape[1]
    step = pl.program_id(0)
    tiles = channels // per_tile

    @pl.when(step == 0)
    def _():
        picked = lax.dot_general(row_ref[...], point_ref[...], NT, preferred_element_type=jnp.float32)
        spread = jnp.dot(
            picked.astype(jnp.bfloat16), column_ref[...], preferred_element_type=jnp.float32
        )
        row = lax.broadcasted_iota(jnp.int32, spread.shape, 0) % cells_y
        column = lax.broadcasted_iota(jnp.int32, spread.shape, 1) % cells_y
        mixing[...] = jnp.where(row == column, spread, 0.0).astype(jnp.bfloat16)

        for r in range(groups):
            own = pl.ds(pl.multiple_of(jnp.bitwise_xor(info_ref[0], r) * rows, 8), rows)
            for j in range(chunks[r].shape[0]):
                modes[own, j * LANES : (j + 1) * LANES] = chunks[r][j].astype(jnp.float32)
        sums = jnp.dot(
            t_ref[0], modes[...].astype(jnp.bfloat16), preferred_element_type=jnp.float32
        )
        cells = sums.shape[0] // 2
        cosine, sine = sums[:cells], sums[cells:]
        wide = sine.shape[1]
        lane = lax.broadcasted_iota(jnp.int32, sine.shape, 1)
        first = lane % (2 * channels) < channels
        turned = jnp.where(
            first, -pltpu.roll(sine, wide - channels, 1), pltpu.roll(sine, channels, 1)
        )
        back = (cosine + turned).astype(jnp.bfloat16)
        ordered = jnp.dot(back, order_ref[...], preferred_element_type=jnp.float32)
        held[...] = ordered.astype(jnp.bfloat16).reshape(held.shape)

    span = tiles * cells_y
    rows = []
    for x in range(here):
        back = held[step * here + x]
        rows += [back[:, k * LANES : (k + 1) * LANES] for k in range(tiles)]
    rows = jnp.concatenate(rows, 0)
    spectral = jnp.dot(
        jnp.concatenate([rows, rows], 1), z_ref[...], preferred_element_type=jnp.float32
    )
    for x in range(here):
        local = jnp.dot(
            mixing[...],
            grad_ref[:, x].reshape(channels * cells_y, length),
            preferred_element_type=jnp.float32,
        )
        for j in range(per_tile):
            both = (
                spectral[x * span : (x + 1) * span, j * length : (j + 1) * length]
                + local[j * span : (j + 1) * span]
            ).astype(jnp.bfloat16)
            for k in range(tiles):
                out_ref[k * per_tile + j, x] = both[k * cells_y : (k + 1) * cells_y]


def inverse(info, chunks, table, order, z_table, point, cell_rows, cell_columns, grad, per_tile, here):
    channels, cells_x, cells_y, length = grad.shape
    block = pl.BlockSpec((channels, here, cells_y, length), lambda i, info: (0, i, 0, 0))
    consts = (order, z_table, point, cell_rows, cell_columns)
    return pl.pallas_call(
        functools.partial(inverse_kernel, len(chunks), per_tile),
        out_shape=jax.ShapeDtypeStruct(grad.shape, jnp.bfloat16),
        grid_spec=pltpu.PrefetchScalarGridSpec(
            num_scalar_prefetch=1,
            grid=(cells_x // here,),
            in_specs=[full(c.shape) for c in chunks]
            + [pl.BlockSpec((1,) + table.shape[1:], lambda i, info: (info[3], 0, 0))]
            + [full(c.shape) for c in consts]
            + [block],
            out_specs=block,
            scratch_shapes=[
                pltpu.VMEM((table.shape[2], order.shape[0]), jnp.float32),
                pltpu.VMEM((cells_x, cells_y, order.shape[1]), jnp.bfloat16),
                pltpu.VMEM((channels * cells_y, channels * cells_y), jnp.bfloat16),
            ],
        ),
        compiler_params=params(32),
        cost_estimate=pl.CostEstimate(
            flops=2 * grad.size * channels * cells_y, bytes_accessed=4 * grad.size, transcendentals=0
        ),
        name="inverse",
    )(info, *chunks, table, *consts, grad)


def flip(value, axes, size, r):
    return lax.ppermute(value, axes, [(i, i ^ r) for i in range(size)])


def body(field_in, grad_pre, spec_weight, point_weight):
    _, channels, cells_x, cells_y, cells_z = field_in.shape
    groups_x, groups_y = lax.axis_size("gx"), lax.axis_size("gy")
    groups, scenes = groups_x * groups_y, lax.axis_size("scene")
    group_axes = ("gx", "gy")
    total_x, total_y = cells_x * groups_x, cells_y * groups_y
    cells = cells_x * cells_y
    norm = float(total_x * total_y * cells_z) ** -0.5
    modes_xd, modes_yd = spec_weight.shape[:2]
    modes = modes_xd * modes_yd
    rows = -(-modes // 8) * 8
    half = LANES // (2 * channels)
    tiles = -(-MZ // half)
    per_quad = -(-tiles // 4)
    kz_pad = 4 * per_quad * half
    block = 8
    slot = 16
    per_tile = LANES // (2 * slot)
    sizes = (groups, groups_y, modes_xd, modes_yd, total_x, total_y)

    me = lax.axis_index(group_axes)
    at_x, at_y = lax.axis_index("gx"), lax.axis_index("gy")
    quad = at_x % 2 * 2 + at_y % 2
    first = at_x // 2 * 2 * groups_y + at_y // 2 * 2
    firsts = [
        x * groups_y + y for x in range(0, groups_x, 2) for y in range(0, groups_y, 2)
    ]
    if len(firsts) * groups * rows * cells * 32 <= 1 << 25:
        forward_t = jnp.asarray(
            np.stack([forward_table(np, f, rows, sizes, cells_x, cells_y) for f in firsts])
        )
        inverse_t = jnp.asarray(
            np.stack([inverse_table(np, i, rows, sizes, cells_x, cells_y) for i in range(groups)])
        )
        forward_at, inverse_at = at_x // 2 * (groups_y // 2) + at_y // 2, me
    else:
        forward_t = forward_table(jnp, first, rows, sizes, cells_x, cells_y)[None]
        inverse_t = inverse_table(jnp, me, rows, sizes, cells_x, cells_y)[None]
        forward_at, inverse_at = 0 * me, 0 * me
    info = jnp.stack([me, quad, forward_at, inverse_at, lax.axis_index("scene")])

    z_table = jnp.asarray(forward_z_table(cells_z, block, kz_pad))
    inverse_z = jnp.asarray(inverse_z_table(cells_z, per_tile, slot, norm))
    order = jnp.asarray(order_table(channels, tiles * half, per_tile, slot))
    lane = np.arange(LANES)
    spread = jnp.asarray(spread_table(channels, half, lane % channels))
    gather = jnp.asarray(gather_table(channels, LANES // channels))
    here = channels // scenes
    pair = np.arange(here * channels)
    pick = jnp.asarray(
        np.stack([spread_table(channels, half, q * here + pair // channels) for q in range(scenes)])
    )
    cell_rows, cell_columns = (jnp.asarray(t) for t in cell_tables(channels, per_tile, cells_y))
    weight_z = np.full((tiles * half, 2 * channels), 2.0 * norm, np.float32)
    weight_z[0] = norm
    grad_scale = jnp.asarray(weight_z.reshape(tiles, 1, LANES))
    field_scale = jnp.full((tiles, 1, LANES), norm, jnp.float32)

    def spectra_of(fields):
        mine = along_z(info, fields, z_table, kz_pad, block)
        cells_of = [mine[0]] + [
            flip(mine[t], group_axes, groups, quad_offset(t, groups_y)) for t in range(1, 4)
        ]
        sums = plane(info, cells_of, forward_t, groups, rows, channels)
        return [sums[0]] + [flip(sums[r], group_axes, groups, r) for r in range(1, groups)]

    grad = grad_pre.reshape(channels, cells, cells_z)
    field = field_in.reshape(channels, cells, cells_z)
    if SPLIT:
        grad_got, field_got, at = spectra_of([grad]), spectra_of([field]), 0
    else:
        grad_got = spectra_of([grad, field])
        field_got, at = grad_got, 1
    weight = spec_weight.reshape(modes, MZ, 2, channels * channels)
    weight = jnp.pad(weight.transpose(1, 2, 0, 3), ((0, 0), (0, 0), (0, rows - modes), (0, 0)))
    grad_sum, mode_grad = mix(
        info, grad_got, 0, grad_scale, weight, spread, gather, groups_y
    )

    gathered = [mode_grad] + [flip(mode_grad, "gy", groups_y, r) for r in range(1, groups_y)]
    for r in range(1, groups_x):
        gathered += [flip(m, "gx", groups_x, r) for m in gathered[:groups_y]]

    field_sum = total(info, field_got, at, field_scale, groups_y)
    both = jnp.stack([field_sum, grad_sum])
    spectra = [both] + [flip(both, "scene", scenes, r) for r in range(1, scenes)]
    grads = outer(info, spectra, spread, pick)
    grad_spec = grads[:MZ, :, :modes].transpose(2, 0, 1, 3)
    grad_spec = grad_spec.reshape(modes_xd, modes_yd, MZ, 2, here * channels)

    grad_field = inverse(
        info,
        gathered,
        inverse_t,
        order,
        inverse_z,
        point_weight,
        cell_rows,
        cell_columns,
        grad_pre.reshape(channels, cells_x, cells_y, cells_z),
        per_tile,
        2,
    )
    return grad_field[None], grad_spec


def solution(mesh):
    return jax.shard_map(
        body,
        mesh=mesh,
        in_specs=(
            P("scene", None, "gx", "gy", None),
            P("scene", None, "gx", "gy", None),
            P("gx", "gy", None, None, None),
            P(),
        ),
        out_specs=(P("scene", None, "gx", "gy", None), P("gx", "gy", None, None, "scene")),
        check_vma=False,
    )
```

```python
import functools
import math

import jax
import jax.numpy as jnp
import ml_dtypes
import numpy as np
from jax import lax
from jax.experimental import pallas as pl
from jax.experimental.pallas import tpu as pltpu
from jax.sharding import PartitionSpec as P

MX = 24
MY = 24
MZ = 13
LANES = 128
NT = (((1,), (1,)), ((), ()))
BF16 = ml_dtypes.bfloat16


def angles(xp, index, modes, positions, length):
    freq = xp.where(index < modes // 2, index, index - modes)
    turns = (freq[..., None] * positions) % length
    return turns.astype(np.float32) * np.float32(2.0 * math.pi / length)


def mode_angles(xp, rows, sizes, local_x, local_y):
    groups, groups_y, modes_xd, modes_yd, total_x, total_y = sizes
    owner = xp.repeat(xp.arange(groups, dtype=np.int32), rows)
    within = xp.tile(xp.arange(rows, dtype=np.int32), groups)
    kx = owner // groups_y * modes_xd + xp.minimum(within // modes_yd, modes_xd - 1)
    ky = owner % groups_y * modes_yd + within % modes_yd
    angle_x = angles(xp, kx, MX, local_x, total_x)
    angle_y = angles(xp, ky, MY, local_y, total_y)
    theta = (angle_x[:, :, None] + angle_y[:, None, :]).reshape(owner.shape[0], -1)
    return theta, (within < modes_xd * modes_yd)[:, None]


def device_cells(xp, me, groups_y, cells_x, cells_y):
    local_x = me // groups_y * cells_x + xp.arange(cells_x, dtype=np.int32)
    local_y = me % groups_y * cells_y + xp.arange(cells_y, dtype=np.int32)
    return local_x, local_y


def forward_table(rows, sizes, cells_x, cells_y):
    groups, groups_y = sizes[:2]
    theta, real = mode_angles(
        np, rows, sizes, *device_cells(np, np.int32(0), groups_y, cells_x, cells_y)
    )
    base = np.where(real, np.concatenate([np.cos(theta), np.sin(theta)], 1), np.float32(0))
    turns = []
    for x in range(0, groups // groups_y, 2):
        for y in range(0, groups_y, 2):
            turn = np.zeros((groups * rows, LANES), np.float32)
            for t in range(4):
                device = np.int32(x * groups_y + y + quad_offset(t, groups_y))
                local_x, local_y = device_cells(np, device, groups_y, cells_x, cells_y)
                angle, _ = mode_angles(np, rows, sizes, local_x[:1], local_y[:1])
                turn[:, 2 * t] = np.cos(angle[:, 0])
                turn[:, 2 * t + 1] = np.sin(angle[:, 0])
            turns.append(turn)
    return base, np.stack(turns)


def inverse_table(xp, me, rows, sizes, cells_x, cells_y):
    theta, real = mode_angles(
        xp, rows, sizes, *device_cells(xp, me, sizes[1], cells_x, cells_y)
    )
    cosine = xp.where(real, xp.cos(theta), np.float32(0))
    sine = xp.where(real, xp.sin(theta), np.float32(0))
    return xp.concatenate([cosine.T, sine.T], 0).astype(BF16)


def quad_offset(t, groups_y):
    return t // 2 * groups_y + t % 2


def quad_of(r, groups_y):
    return r // groups_y % 2 * 2 + r % groups_y % 2


def z_angles(length):
    return angles(np, np.arange(MZ, dtype=np.int32), 2 * MZ, np.arange(length, dtype=np.int32), length)


def forward_z_table(length):
    theta = z_angles(length)
    parts = np.stack([np.cos(theta), -np.sin(theta)], 1).reshape(2 * MZ, length)
    table = np.zeros((-(-2 * MZ // 16) * 16, length), np.float32)
    table[: 2 * MZ] = parts
    return table.astype(BF16)


def split16(values):
    high = values.astype(BF16)
    low = (values - high.astype(np.float32)).astype(BF16)
    return high, low


def inverse_z_table(length, per_tile, slot, norm):
    theta = z_angles(length)
    parts = np.stack([np.cos(theta), -np.sin(theta)], 0) * np.float32(norm)
    table = np.zeros((per_tile, 2, slot, per_tile, length), np.float32)
    for c in range(per_tile):
        table[c, :, :MZ, c] = parts
    high, low = split16(table.reshape(LANES, per_tile * length))
    return np.concatenate([high, low], 0)


def order_table(channels, kz_pad, per_tile, slot):
    table = np.zeros((kz_pad, 2, channels, channels // per_tile, per_tile, 2, slot), np.float32)
    for kz in range(MZ):
        for part in range(2):
            for c in range(channels):
                table[kz, part, c, c // per_tile, c % per_tile, part, kz] = 1
    return table.reshape(kz_pad * 2 * channels, -1).astype(BF16)


def spread_table(channels, half, copies):
    table = np.zeros((half, 2, channels, half, 2, copies.shape[0]), np.float32)
    for h in range(half):
        for part in range(2):
            table[h, part, copies, h, part, np.arange(copies.shape[0])] = 1
    return table.reshape(half * 2 * channels, -1).astype(BF16)


def gather_table(channels, copies):
    table = np.zeros((channels, channels, copies, channels), np.float32)
    for i in range(channels):
        table[i, :, :, i] = 1
    return table.reshape(channels * channels, -1).astype(BF16)


def cell_tables(channels, per_tile, cells_y):
    rows = np.zeros((per_tile, channels // per_tile, cells_y, channels), np.float32)
    for c in range(channels):
        rows[c % per_tile, c // per_tile, :, c] = 1
    columns = np.repeat(np.eye(channels, dtype=np.float32), cells_y, 1)
    return rows.reshape(-1, channels).astype(BF16), columns.astype(BF16)


def regroup_table(channels, block, half):
    groups = channels // block
    kz_tile = LANES // (2 * block)
    table = np.zeros((groups, kz_tile, 2, block, kz_tile // half, half, 2, groups, block), np.float32)
    for g in range(groups):
        for kz in range(kz_tile):
            for part in range(2):
                for c in range(block):
                    table[g, kz, part, c, kz // half, kz % half, part, g, c] = 1
    return table.reshape(groups * LANES, -1).astype(BF16)


def params(mib):
    return pltpu.CompilerParams(vmem_limit_bytes=mib * 1024 * 1024)


IN_VMEM = pl.BlockSpec(memory_space=pltpu.VMEM)
IN_SMEM = pl.BlockSpec(memory_space=pltpu.SMEM)
IN_HBM = pl.BlockSpec(memory_space=pl.ANY)


def resident(*arrays):
    return [pltpu.with_memory_space_constraint(a, pltpu.VMEM) for a in arrays]


def along_z_kernel(info_ref, z_ref, x_ref, *rest):
    outs, table = rest[:4], rest[4]
    block, span, _ = table.shape
    shape = (span, z_ref.shape[0])
    row = lax.broadcasted_iota(jnp.int32, shape, 0) // block
    repeat = (row == lax.broadcasted_iota(jnp.int32, shape, 1)).astype(jnp.bfloat16)
    rows = jnp.dot(repeat, z_ref[...], preferred_element_type=jnp.float32)
    channel = lax.broadcasted_iota(jnp.int32, rows.shape, 0) % block
    for c in range(block):
        table[c] = jnp.where(channel == c, rows, 0.0).astype(jnp.bfloat16)
    for t in range(4):
        first = jnp.bitwise_xor(info_ref[1], t) * block
        total = None
        for c in range(block):
            term = lax.dot_general(
                table[c], x_ref[first + c], NT, preferred_element_type=jnp.float32
            )
            total = term if total is None else total + term
        outs[t][...] = total.astype(jnp.bfloat16)


def along_z(info, field, z_table, block):
    channels, cells, length = field.shape
    span = 2 * MZ * block
    return pl.pallas_call(
        along_z_kernel,
        out_shape=[jax.ShapeDtypeStruct((span, cells), jnp.bfloat16)] * 4,
        in_specs=[IN_SMEM] + [IN_VMEM] * 2,
        out_specs=[IN_VMEM] * 4,
        scratch_shapes=[pltpu.VMEM((block, span, length), jnp.bfloat16)],
        compiler_params=params(12),
        cost_estimate=pl.CostEstimate(
            flops=2 * span * cells * length * channels,
            bytes_accessed=2 * field.size,
            transcendentals=0,
        ),
        name="along_z",
    )(info, *resident(z_table, field))


def place_cells(info_ref, sources, block, data):
    span, cells = sources[0].shape
    for t in range(4):
        place = jnp.bitwise_xor(info_ref[1], t)
        value = sources[t][...].astype(jnp.float32)
        turned = []
        for k in range(0, span, 2 * block):
            turned += [value[k + block : k + 2 * block], -value[k : k + block]]
        data[place, :, :cells] = sources[t][...]
        data[place, :, cells:] = jnp.concatenate(turned, 0).astype(jnp.bfloat16)


def sum_plane(table, data):
    total = None
    for device in range(4):
        for part in range(2):
            term = lax.dot_general(
                table[device, part], data[device], NT, preferred_element_type=jnp.float32
            )
            total = term if total is None else total + term
    return total


def first_plane_kernel(block, info_ref, base_ref, turn_ref, *refs):
    sources, (out_ref, table, data) = refs[:4], refs[4:]
    cells = sources[0].shape[1]
    place_cells(info_ref, sources, block, data)
    turns = turn_ref[info_ref[2]]
    cosine, sine = base_ref[:, :cells], base_ref[:, cells:]
    for device in range(4):
        turn_cos = turns[:, 2 * device : 2 * device + 1]
        turn_sin = turns[:, 2 * device + 1 : 2 * device + 2]
        both = (cosine * turn_cos - sine * turn_sin, sine * turn_cos + cosine * turn_sin)
        for k, values in enumerate(both):
            high = values.astype(jnp.bfloat16)
            table[device, 0, :, k * cells : (k + 1) * cells] = high
            low = (values - high.astype(jnp.float32)).astype(jnp.bfloat16)
            table[device, 1, :, k * cells : (k + 1) * cells] = low
    out_ref[...] = sum_plane(table, data)


def first_plane(info, sources, base, turns, block):
    span, cells = sources[0].shape
    modes = base.shape[0]
    return pl.pallas_call(
        functools.partial(first_plane_kernel, block),
        out_shape=[
            jax.ShapeDtypeStruct((modes, span), jnp.float32),
            jax.ShapeDtypeStruct((4, 2, modes, 2 * cells), jnp.bfloat16),
        ],
        in_specs=[IN_SMEM] + [IN_VMEM] * 6,
        out_specs=[IN_VMEM] * 2,
        scratch_shapes=[pltpu.VMEM((4, span, 2 * cells), jnp.bfloat16)],
        compiler_params=params(24),
        cost_estimate=pl.CostEstimate(
            flops=32 * cells * span * modes, bytes_accessed=4 * base.size, transcendentals=0
        ),
        name="first_plane",
    )(info, *resident(base, turns), *sources)


def tail_parts(rows):
    return next(k for k in (3, 2, 1) if rows % (8 * k) == 0)


def second_plane_kernel(groups, rows, block, info_ref, table_ref, other_ref, *refs):
    sources, outs, (sums, data) = refs[:4], refs[4 : 4 + groups], refs[4 + groups :]
    place_cells(info_ref, sources, block, data)
    sums[...] = sum_plane(table_ref, data)
    over = sums.shape[1] - LANES
    room = LANES - over
    parts = tail_parts(rows)
    step = rows // parts
    for r in range(groups):
        owner = jnp.bitwise_xor(info_ref[0], r)
        own = pl.ds(pl.multiple_of(owner * rows, 8), rows)
        first, second = other_ref[own], sums[own]
        mixed = jnp.concatenate([first[:, LANES:], second[:, LANES : LANES + room]], 1)
        tail = second[:, LANES + room :]
        tail = [tail[k * step : (k + 1) * step] for k in range(parts)]
        rest = LANES - parts * (over - room)
        tail = jnp.concatenate(tail + [jnp.zeros((step, rest), jnp.float32)], 1)
        whole = jnp.concatenate([first[:, :LANES], second[:, :LANES], mixed, tail], 0)
        outs[r][...] = whole.astype(jnp.bfloat16)


def second_plane(info, sources, table, other, groups, rows, block):
    span, cells = sources[0].shape
    modes = table.shape[2]
    chunk = jax.ShapeDtypeStruct((3 * rows + rows // tail_parts(rows), LANES), jnp.bfloat16)
    return pl.pallas_call(
        functools.partial(second_plane_kernel, groups, rows, block),
        out_shape=[chunk] * groups,
        in_specs=[IN_SMEM] + [IN_VMEM] * 6,
        out_specs=[IN_VMEM] * groups,
        scratch_shapes=[
            pltpu.VMEM((modes, span), jnp.float32),
            pltpu.VMEM((4, span, 2 * cells), jnp.bfloat16),
        ],
        compiler_params=params(24),
        cost_estimate=pl.CostEstimate(
            flops=32 * cells * span * modes, bytes_accessed=2 * table.size, transcendentals=0
        ),
        name="second_plane",
    )(info, *resident(table), other, *sources)


def total_kernel(groups, groups_y, over, scale, info_ref, scale_ref, regroup_ref, *refs):
    chunks, outs, held = refs[:groups], refs[groups:-1], refs[-1]
    rows = held.shape[2]
    parts = tail_parts(rows)
    room = LANES - over
    left = over - room
    for t in range(4):
        place = jnp.bitwise_xor(info_ref[1], t)
        mine = [c for r, c in enumerate(chunks) if quad_of(r, groups_y) == t]
        total = mine[0][...].astype(jnp.float32)
        for ref in mine[1:]:
            total = total + ref[...].astype(jnp.float32)
        mixed, tail = total[2 * rows : 3 * rows], total[3 * rows :]
        tail = jnp.concatenate([tail[:, k * left : (k + 1) * left] for k in range(parts)], 0)
        zeros = jnp.zeros((rows, room), jnp.float32)
        held[place, 0] = total[:rows]
        held[place, 1] = jnp.concatenate([mixed[:, :over], zeros], 1)
        held[place, 2] = total[rows : 2 * rows]
        held[place, 3] = jnp.concatenate([mixed[:, over:], tail, zeros], 1)
    tiles = outs[0].shape[0] - 2
    for j in range(2):
        values = jnp.concatenate([held[g, j] for g in range(4)], 1) * scale_ref[j : j + 1]
        sums = jnp.dot(
            values.astype(jnp.bfloat16), regroup_ref[...], preferred_element_type=jnp.float32
        ).astype(jnp.bfloat16)
        for k in range(4):
            if j * 4 + k < tiles:
                for out in outs:
                    out[j * 4 + k] = sums[:, k * LANES : (k + 1) * LANES]
    for r, out in enumerate(outs):
        for j in range(2):
            value = held[jnp.bitwise_xor(info_ref[4], r), 2 + j] * scale
            out[tiles + j] = value.astype(jnp.bfloat16)


def total(info, chunks, scale, norm, regroup, tiles, rows, over, scenes, groups_y):
    out = jax.ShapeDtypeStruct((tiles + 2, rows, LANES), jnp.bfloat16)
    return pl.pallas_call(
        functools.partial(total_kernel, len(chunks), groups_y, over, norm),
        out_shape=[out] * scenes,
        in_specs=[IN_SMEM] + [IN_VMEM] * (2 + len(chunks)),
        out_specs=[IN_VMEM] * scenes,
        scratch_shapes=[pltpu.VMEM((4, 4, rows, LANES), jnp.float32)],
        compiler_params=params(12),
        cost_estimate=pl.CostEstimate(
            flops=4 * rows * regroup.size,
            bytes_accessed=2 * len(chunks) * chunks[0].size,
            transcendentals=0,
        ),
        name="total",
    )(info, *resident(scale, regroup), *chunks)


def mix_kernel(spread_ref, gather_ref, w_ref, s_ref, out_ref):
    tiles, rows, _ = out_ref.shape
    last, _, _, width = w_ref.shape
    half = spread_ref.shape[1] // (2 * LANES)
    for tile in range(tiles):
        wide = jnp.dot(s_ref[tile], spread_ref[...], preferred_element_type=jnp.float32)
        products = []
        for h in range(half):
            kz = tile * half + h
            if kz >= last:
                continue
            out_re = wide[:, (2 * h) * LANES : (2 * h + 1) * LANES]
            out_im = wide[:, (2 * h + 1) * LANES : (2 * h + 2) * LANES]
            real, imag = [], []
            for k in range(width // LANES):
                lane = slice(k * LANES, (k + 1) * LANES)
                w_re = w_ref[kz, 0, :, lane].astype(jnp.float32)
                w_im = w_ref[kz, 1, :, lane].astype(jnp.float32)
                real.append((w_re * out_re + w_im * out_im).astype(jnp.bfloat16))
                imag.append((w_re * out_im - w_im * out_re).astype(jnp.bfloat16))
            products += [jnp.concatenate(real, 1), jnp.concatenate(imag, 1)]
        sums = jnp.dot(
            jnp.concatenate(products, 0), gather_ref[...], preferred_element_type=jnp.float32
        )
        which = lax.broadcasted_iota(jnp.int32, (rows, LANES), 1) // (LANES // (2 * half))
        out = sums[:rows]
        for k in range(1, len(products)):
            out = jnp.where(which == k, sums[k * rows : (k + 1) * rows], out)
        out_ref[tile] = jnp.where(which < len(products), out, 0.0).astype(jnp.bfloat16)


def mix(spectra, weight, spread, gather):
    tiles, rows = spectra.shape[0] - 2, spectra.shape[1]
    return pl.pallas_call(
        mix_kernel,
        out_shape=jax.ShapeDtypeStruct((tiles, rows, LANES), jnp.bfloat16),
        in_specs=[IN_VMEM] * 4,
        out_specs=IN_VMEM,
        compiler_params=params(16),
        cost_estimate=pl.CostEstimate(
            flops=8 * tiles * rows * gather.size, bytes_accessed=2 * weight.size, transcendentals=0
        ),
        name="mix",
    )(*resident(spread, gather, weight), spectra)


def outer_kernel(scenes, spread_ref, pick_ref, *refs):
    spectra, out_ref = refs[:scenes], refs[scenes]
    last, _, rows, wide = out_ref.shape
    half = spread_ref.shape[1] // (2 * LANES)
    per_tile = pick_ref.shape[0]
    tiles = spectra[0].shape[0] - 2
    for kz in range(last):
        if kz % half == 0:
            grads = jnp.dot(
                jnp.concatenate([ref[kz // half] for ref in spectra], 0),
                spread_ref[...],
                preferred_element_type=jnp.float32,
            )
        if kz % per_tile == 0:
            field = jnp.concatenate([ref[tiles + kz // per_tile] for ref in spectra], 0)
        hats = jnp.dot(field, pick_ref[kz % per_tile], preferred_element_type=jnp.float32)
        lane = 2 * (kz % half) * LANES
        for k in range(wide // LANES):
            real, imag = 0.0, 0.0
            for s in range(scenes):
                here = slice(s * rows, (s + 1) * rows)
                hat_re = hats[here, k * LANES : (k + 1) * LANES]
                hat_im = hats[here, wide + k * LANES : wide + (k + 1) * LANES]
                out_re = grads[here, lane : lane + LANES]
                out_im = grads[here, lane + LANES : lane + 2 * LANES]
                real += out_re * hat_re + out_im * hat_im
                imag += out_im * hat_re - out_re * hat_im
            out_ref[kz, 0, :, k * LANES : (k + 1) * LANES] = real
            out_ref[kz, 1, :, k * LANES : (k + 1) * LANES] = imag


def outer(spectra, spread, pick):
    tiles, rows, _ = spectra[0].shape
    wide = pick.shape[2] // 2
    return pl.pallas_call(
        functools.partial(outer_kernel, len(spectra)),
        out_shape=jax.ShapeDtypeStruct((MZ, 2, rows, wide), jnp.float32),
        in_specs=[IN_VMEM] * (2 + len(spectra)),
        out_specs=IN_VMEM,
        compiler_params=params(16),
        cost_estimate=pl.CostEstimate(
            flops=2 * tiles * rows * 4 * LANES * 12 * LANES,
            bytes_accessed=16 * tiles * rows * wide + 8 * tiles * rows * LANES * len(spectra),
            transcendentals=0,
        ),
        name="outer",
    )(*resident(spread, pick), *spectra)


def local_kernel(row_ref, column_ref, point_ref, grad_ref, out_ref, mixing):
    channels, cells_x, cells_y, length = grad_ref.shape
    picked = lax.dot_general(row_ref[...], point_ref[...], NT, preferred_element_type=jnp.float32)
    spread = jnp.dot(
        picked.astype(jnp.bfloat16), column_ref[...], preferred_element_type=jnp.float32
    )
    row = lax.broadcasted_iota(jnp.int32, spread.shape, 0) % cells_y
    column = lax.broadcasted_iota(jnp.int32, spread.shape, 1) % cells_y
    mixing[...] = jnp.where(row == column, spread, 0.0).astype(jnp.bfloat16)

    @pl.loop(0, cells_x)
    def _(x):
        out_ref[x] = jnp.dot(
            mixing[...],
            grad_ref[:, x].reshape(channels * cells_y, length),
            preferred_element_type=jnp.float32,
        ).astype(out_ref.dtype)


def local(cell_rows, cell_columns, point, grad):
    channels, cells_x, cells_y, length = grad.shape
    width = channels * cells_y
    return pl.pallas_call(
        local_kernel,
        out_shape=jax.ShapeDtypeStruct((cells_x, width, length), jnp.bfloat16),
        in_specs=[IN_VMEM] * 4,
        out_specs=IN_VMEM,
        scratch_shapes=[pltpu.VMEM((width, width), jnp.bfloat16)],
        compiler_params=params(16),
        cost_estimate=pl.CostEstimate(
            flops=2 * grad.size * width, bytes_accessed=4 * grad.size, transcendentals=0
        ),
        name="local",
    )(*resident(cell_rows, cell_columns, point, grad))


def inverse_kernel(groups, per_tile, here, info_ref, t_ref, order_ref, z_ref, local_ref, *refs):
    chunks, (out_ref, modes, held, built, sems) = refs[:groups], refs[groups:]
    channels, cells_x, cells_y, length = built.shape
    rows = chunks[0].shape[1]
    tiles = channels // per_tile
    for r in range(groups):
        own = pl.ds(pl.multiple_of(jnp.bitwise_xor(info_ref[0], r) * rows, 8), rows)
        for j in range(chunks[r].shape[0]):
            modes[own, j * LANES : (j + 1) * LANES] = chunks[r][j].astype(jnp.float32)
    sums = jnp.dot(
        t_ref[info_ref[3]], modes[...].astype(jnp.bfloat16), preferred_element_type=jnp.float32
    )
    cells = sums.shape[0] // 2
    cosine, sine = sums[:cells], sums[cells:]
    wide = sine.shape[1]
    lane = lax.broadcasted_iota(jnp.int32, sine.shape, 1)
    first = lane % (2 * channels) < channels
    turned = jnp.where(
        first, -pltpu.roll(sine, wide - channels, 1), pltpu.roll(sine, channels, 1)
    )
    back = (cosine + turned).astype(jnp.bfloat16)
    ordered = jnp.dot(back, order_ref[...], preferred_element_type=jnp.float32)
    held[...] = ordered.astype(jnp.bfloat16).reshape(held.shape)

    span = tiles * cells_y
    copies = []
    for start in range(0, cells_x, here):
        stack = []
        for x in range(start, start + here):
            back = held[x]
            stack += [back[:, k * LANES : (k + 1) * LANES] for k in range(tiles)]
        stack = jnp.concatenate(stack, 0)
        spectral = jnp.dot(
            jnp.concatenate([stack, stack], 1), z_ref[...], preferred_element_type=jnp.float32
        )
        for x in range(here):
            for j in range(per_tile):
                both = (
                    spectral[x * span : (x + 1) * span, j * length : (j + 1) * length]
                    + local_ref[start + x, j * span : (j + 1) * span].astype(jnp.float32)
                ).astype(jnp.bfloat16)
                for k in range(tiles):
                    built[k * per_tile + j, start + x] = both[k * cells_y : (k + 1) * cells_y]
        copies.append(
            pltpu.make_async_copy(
                built.at[:, pl.ds(start, here)],
                out_ref.at[:, pl.ds(start, here)],
                sems.at[start // here],
            )
        )
        copies[-1].start()
    for copy in copies:
        copy.wait()


def inverse(info, chunks, table, order, z_table, local_part, shape, per_tile, here):
    channels, cells_x, cells_y, length = shape
    return pl.pallas_call(
        functools.partial(inverse_kernel, len(chunks), per_tile, here),
        out_shape=jax.ShapeDtypeStruct(shape, jnp.bfloat16),
        in_specs=[IN_SMEM] + [IN_VMEM] * (4 + len(chunks)),
        out_specs=IN_HBM,
        scratch_shapes=[
            pltpu.VMEM((table.shape[2], order.shape[0]), jnp.float32),
            pltpu.VMEM((cells_x, cells_y, order.shape[1]), jnp.bfloat16),
            pltpu.VMEM(shape, jnp.bfloat16),
            pltpu.SemaphoreType.DMA((cells_x // here,)),
        ],
        compiler_params=params(28),
        cost_estimate=pl.CostEstimate(
            flops=2 * local_part.size * LANES, bytes_accessed=4 * local_part.size, transcendentals=0
        ),
        name="inverse",
    )(info, *resident(table, order, z_table, local_part), *chunks)


def flip(value, axes, size, r):
    return lax.ppermute(value, axes, [(i, i ^ r) for i in range(size)])


def body(field_in, grad_pre, spec_weight, point_weight):
    _, channels, cells_x, cells_y, cells_z = field_in.shape
    groups_x, groups_y = lax.axis_size("gx"), lax.axis_size("gy")
    groups, scenes = groups_x * groups_y, lax.axis_size("scene")
    group_axes = ("gx", "gy")
    total_x, total_y = cells_x * groups_x, cells_y * groups_y
    cells = cells_x * cells_y
    norm = float(total_x * total_y * cells_z) ** -0.5
    modes_xd, modes_yd = spec_weight.shape[:2]
    modes = modes_xd * modes_yd
    rows = -(-modes // 8) * 8
    half = LANES // (2 * channels)
    tiles = -(-MZ // half)
    block = channels // 4
    slot = 16
    per_tile = LANES // (2 * slot)
    sizes = (groups, groups_y, modes_xd, modes_yd, total_x, total_y)

    me = lax.axis_index(group_axes)
    at_x, at_y = lax.axis_index("gx"), lax.axis_index("gy")
    quad = at_x % 2 * 2 + at_y % 2
    base, turns = (jnp.asarray(t) for t in forward_table(rows, sizes, cells_x, cells_y))
    if groups * groups * rows * 2 * cells <= 1 << 24:
        inverse_t = jnp.asarray(
            np.stack([inverse_table(np, i, rows, sizes, cells_x, cells_y) for i in range(groups)])
        )
        inverse_at = me
    else:
        inverse_t = inverse_table(jnp, me, rows, sizes, cells_x, cells_y)[None]
        inverse_at = 0 * me
    forward_at = at_x // 2 * (groups_y // 2) + at_y // 2
    info = jnp.stack([me, quad, forward_at, inverse_at, lax.axis_index("scene")])

    z_table = jnp.asarray(forward_z_table(cells_z))
    regroup = jnp.asarray(regroup_table(channels, block, half))
    inverse_z = jnp.asarray(inverse_z_table(cells_z, per_tile, slot, norm))
    order = jnp.asarray(order_table(channels, tiles * half, per_tile, slot))
    lane = np.arange(LANES)
    spread = jnp.asarray(spread_table(channels, half, lane % channels))
    gather = jnp.asarray(gather_table(channels, LANES // channels))
    here = channels // scenes
    pair = np.arange(here * channels)
    kz_tile = LANES // (2 * block)
    pick = spread_table(here, kz_tile, pair // channels).reshape(LANES, kz_tile, -1)
    pick = jnp.asarray(pick.transpose(1, 0, 2))
    cell_rows, cell_columns = (jnp.asarray(t) for t in cell_tables(channels, per_tile, cells_y))
    scale = np.full((2, 4, kz_tile, 2 * block), 2.0 * norm, np.float32)
    scale[0, :, 0] = norm
    scale = jnp.asarray(scale.reshape(2, 4 * LANES))

    def cells_of(field):
        mine = along_z(info, field.reshape(channels, cells, cells_z), z_table, block)
        return [mine[0]] + [
            flip(mine[t], group_axes, groups, quad_offset(t, groups_y)) for t in range(1, 4)
        ]

    grad_cells = cells_of(grad_pre)
    field, _ = lax.optimization_barrier((field_in, grad_cells[0]))
    field_cells = cells_of(field)
    grad_sums, table = first_plane(info, grad_cells, base, turns, block)
    sums = second_plane(info, field_cells, table, grad_sums, groups, rows, block)
    got = [sums[0]] + [flip(sums[r], group_axes, groups, r) for r in range(1, groups)]
    weight = spec_weight.reshape(modes, MZ, 2, channels * channels)
    weight = jnp.pad(weight.transpose(1, 2, 0, 3), ((0, 0), (0, 0), (0, rows - modes), (0, 0)))
    local_part = local(
        cell_rows,
        cell_columns,
        point_weight,
        grad_pre.reshape(channels, cells_x, cells_y, cells_z),
    )
    got, weight, local_part = lax.optimization_barrier((got, weight, local_part))
    over = 2 * MZ * block - LANES
    spectra = total(
        info, got, scale, norm, regroup, tiles, rows, over, scenes, groups_y
    )
    mode_grad = mix(spectra[0], weight, spread, gather)

    along_y = {0: mode_grad}
    apart = groups_y // 2
    while apart:
        along_y.update({r ^ apart: flip(v, "gy", groups_y, apart) for r, v in along_y.items()})
        apart //= 2
    gathered = [along_y[r] for r in range(groups_y)]
    for r in range(1, groups_x):
        gathered += [flip(m, "gx", groups_x, r) for m in gathered[:groups_y]]

    others, _ = lax.optimization_barrier((spectra[1:], mode_grad))
    spectra = [spectra[0]] + [flip(others[r - 1], "scene", scenes, r) for r in range(1, scenes)]
    grads = outer(spectra, spread, pick)
    grad_spec = grads[:, :, :modes].transpose(2, 0, 1, 3)
    grad_spec = grad_spec.reshape(modes_xd, modes_yd, MZ, 2, here * channels)

    gathered, grad_spec = lax.optimization_barrier((gathered, grad_spec))
    grad_field = inverse(
        info,
        gathered,
        inverse_t,
        order,
        inverse_z,
        local_part,
        (channels, cells_x, cells_y, cells_z),
        per_tile,
        2,
    )
    return grad_field[None], grad_spec


def solution(mesh):
    return jax.shard_map(
        body,
        mesh=mesh,
        in_specs=(
            P("scene", None, "gx", "gy", None),
            P("scene", None, "gx", "gy", None),
            P("gx", "gy", None, None, None),
            P(),
        ),
        out_specs=(P("scene", None, "gx", "gy", None), P("gx", "gy", None, None, "scene")),
        check_vma=False,
    )
```

```python
import functools
import math

import jax
import jax.numpy as jnp
import ml_dtypes
import numpy as np
from jax import lax
from jax.experimental import pallas as pl
from jax.experimental.pallas import tpu as pltpu
from jax.sharding import PartitionSpec as P

MX = 24
MY = 24
MZ = 13
LANES = 128
NT = (((1,), (1,)), ((), ()))
BF16 = ml_dtypes.bfloat16


def angles(xp, index, modes, positions, length):
    freq = xp.where(index < modes // 2, index, index - modes)
    turns = (freq[..., None] * positions) % length
    return turns.astype(np.float32) * np.float32(2.0 * math.pi / length)


def mode_angles(xp, rows, sizes, local_x, local_y):
    groups, groups_y, modes_xd, modes_yd, total_x, total_y = sizes
    owner = xp.repeat(xp.arange(groups, dtype=np.int32), rows)
    within = xp.tile(xp.arange(rows, dtype=np.int32), groups)
    kx = owner // groups_y * modes_xd + xp.minimum(within // modes_yd, modes_xd - 1)
    ky = owner % groups_y * modes_yd + within % modes_yd
    angle_x = angles(xp, kx, MX, local_x, total_x)
    angle_y = angles(xp, ky, MY, local_y, total_y)
    theta = (angle_x[:, :, None] + angle_y[:, None, :]).reshape(owner.shape[0], -1)
    return theta, (within < modes_xd * modes_yd)[:, None]


def device_cells(xp, me, groups_y, cells_x, cells_y):
    local_x = me // groups_y * cells_x + xp.arange(cells_x, dtype=np.int32)
    local_y = me % groups_y * cells_y + xp.arange(cells_y, dtype=np.int32)
    return local_x, local_y


def forward_table(rows, sizes, cells_x, cells_y):
    groups, groups_y = sizes[:2]
    theta, real = mode_angles(
        np, rows, sizes, *device_cells(np, np.int32(0), groups_y, cells_x, cells_y)
    )
    base = np.where(real, np.concatenate([np.cos(theta), np.sin(theta)], 1), np.float32(0))
    turns = []
    for x in range(0, groups // groups_y, 2):
        for y in range(0, groups_y, 2):
            turn = np.zeros((groups * rows, LANES), np.float32)
            for t in range(4):
                device = np.int32(x * groups_y + y + quad_offset(t, groups_y))
                local_x, local_y = device_cells(np, device, groups_y, cells_x, cells_y)
                angle, _ = mode_angles(np, rows, sizes, local_x[:1], local_y[:1])
                turn[:, 2 * t] = np.cos(angle[:, 0])
                turn[:, 2 * t + 1] = np.sin(angle[:, 0])
            turns.append(turn)
    return base, np.stack(turns)


def inverse_table(xp, me, rows, sizes, cells_x, cells_y):
    theta, real = mode_angles(
        xp, rows, sizes, *device_cells(xp, me, sizes[1], cells_x, cells_y)
    )
    cosine = xp.where(real, xp.cos(theta), np.float32(0))
    sine = xp.where(real, xp.sin(theta), np.float32(0))
    return xp.concatenate([cosine.T, sine.T], 0).astype(BF16)


def quad_offset(t, groups_y):
    return t // 2 * groups_y + t % 2


def quad_of(r, groups_y):
    return r // groups_y % 2 * 2 + r % groups_y % 2


def split16(values):
    high = values.astype(BF16)
    low = (values - high.astype(np.float32)).astype(BF16)
    return high, low


def inverse_z_table(length, per_tile, slot, norm):
    modes, cells = np.arange(MZ, dtype=np.int32), np.arange(length, dtype=np.int32)
    theta = angles(np, modes, 2 * MZ, cells, length)
    parts = np.stack([np.cos(theta), -np.sin(theta)], 0) * np.float32(norm)
    table = np.zeros((per_tile, 2, slot, per_tile, length), np.float32)
    for c in range(per_tile):
        table[c, :, :MZ, c] = parts
    high, low = split16(table.reshape(LANES, per_tile * length))
    return np.concatenate([high, low], 0)


def order_table(channels, kz_pad, per_tile, slot):
    table = np.zeros((kz_pad, 2, channels, channels // per_tile, per_tile, 2, slot), np.float32)
    for kz in range(MZ):
        for part in range(2):
            for c in range(channels):
                table[kz, part, c, c // per_tile, c % per_tile, part, kz] = 1
    return table.reshape(kz_pad * 2 * channels, -1).astype(BF16)


def spread_table(channels, half, copies):
    table = np.zeros((half, 2, channels, half, 2, copies.shape[0]), np.float32)
    for h in range(half):
        for part in range(2):
            table[h, part, copies, h, part, np.arange(copies.shape[0])] = 1
    return table.reshape(half * 2 * channels, -1).astype(BF16)


def gather_table(channels, copies):
    table = np.zeros((channels, channels, copies, channels), np.float32)
    for i in range(channels):
        table[i, :, :, i] = 1
    return table.reshape(channels * channels, -1).astype(BF16)


def cell_tables(channels, per_tile, cells_y):
    rows = np.zeros((per_tile, channels // per_tile, cells_y, channels), np.float32)
    for c in range(channels):
        rows[c % per_tile, c // per_tile, :, c] = 1
    columns = np.repeat(np.eye(channels, dtype=np.float32), cells_y, 1)
    return rows.reshape(-1, channels).astype(BF16), columns.astype(BF16)


def regroup_table(channels, block, half):
    groups = channels // block
    kz_tile = LANES // (2 * block)
    table = np.zeros((groups, kz_tile, 2, block, kz_tile // half, half, 2, groups, block), np.float32)
    for g in range(groups):
        for kz in range(kz_tile):
            for part in range(2):
                for c in range(block):
                    table[g, kz, part, c, kz // half, kz % half, part, g, c] = 1
    return table.reshape(groups * LANES, -1).astype(BF16)


def params(mib):
    return pltpu.CompilerParams(vmem_limit_bytes=mib * 1024 * 1024)


IN_VMEM = pl.BlockSpec(memory_space=pltpu.VMEM)
IN_SMEM = pl.BlockSpec(memory_space=pltpu.SMEM)
IN_HBM = pl.BlockSpec(memory_space=pl.ANY)


def resident(*arrays):
    return [pltpu.with_memory_space_constraint(a, pltpu.VMEM) for a in arrays]


def along_z_kernel(info_ref, x_ref, *rest):
    outs, table = rest[:4], rest[4]
    block, span, length = table.shape
    padded = -(-2 * MZ // 16) * 16
    row = lax.broadcasted_iota(jnp.int32, (padded, length), 0)
    cell = lax.broadcasted_iota(jnp.int32, (padded, length), 1)
    theta = ((row // 2 * cell) % length).astype(jnp.float32) * (2.0 * math.pi / length)
    parts = jnp.where(row % 2 == 0, jnp.cos(theta), -jnp.sin(theta))
    row = lax.broadcasted_iota(jnp.int32, (span, padded), 0) // block
    repeat = (row == lax.broadcasted_iota(jnp.int32, (span, padded), 1)).astype(jnp.bfloat16)
    rows = jnp.dot(repeat, parts.astype(jnp.bfloat16), preferred_element_type=jnp.float32)
    channel = lax.broadcasted_iota(jnp.int32, rows.shape, 0) % block
    for c in range(block):
        table[c] = jnp.where(channel == c, rows, 0.0).astype(jnp.bfloat16)
    for t in range(4):
        first = jnp.bitwise_xor(info_ref[1], t) * block
        total = None
        for c in range(block):
            term = lax.dot_general(
                table[c], x_ref[first + c], NT, preferred_element_type=jnp.float32
            )
            total = term if total is None else total + term
        outs[t][...] = total.astype(jnp.bfloat16)


def along_z(info, field, block):
    channels, cells, length = field.shape
    span = 2 * MZ * block
    return pl.pallas_call(
        along_z_kernel,
        out_shape=[jax.ShapeDtypeStruct((span, cells), jnp.bfloat16)] * 4,
        in_specs=[IN_SMEM, IN_VMEM],
        out_specs=[IN_VMEM] * 4,
        scratch_shapes=[pltpu.VMEM((block, span, length), jnp.bfloat16)],
        compiler_params=params(12),
        cost_estimate=pl.CostEstimate(
            flops=2 * span * cells * length * channels,
            bytes_accessed=2 * field.size,
            transcendentals=0,
        ),
        name="along_z",
    )(info, *resident(field))


def place_cells(info_ref, sources, block, data):
    span, cells = sources[0].shape
    for t in range(4):
        place = jnp.bitwise_xor(info_ref[1], t)
        value = sources[t][...].astype(jnp.float32)
        turned = []
        for k in range(0, span, 2 * block):
            turned += [value[k + block : k + 2 * block], -value[k : k + block]]
        data[place, :, :cells] = sources[t][...]
        data[place, :, cells:] = jnp.concatenate(turned, 0).astype(jnp.bfloat16)


def sum_plane(table, data):
    total = None
    for device in range(4):
        for part in range(2):
            term = lax.dot_general(
                table[device, part], data[device], NT, preferred_element_type=jnp.float32
            )
            total = term if total is None else total + term
    return total


def first_plane_kernel(block, info_ref, base_ref, turn_ref, *refs):
    sources, (out_ref, table, data) = refs[:4], refs[4:]
    cells = sources[0].shape[1]
    place_cells(info_ref, sources, block, data)
    turns = turn_ref[info_ref[2]]
    cosine, sine = base_ref[:, :cells], base_ref[:, cells:]
    for device in range(4):
        turn_cos = turns[:, 2 * device : 2 * device + 1]
        turn_sin = turns[:, 2 * device + 1 : 2 * device + 2]
        both = (cosine * turn_cos - sine * turn_sin, sine * turn_cos + cosine * turn_sin)
        for k, values in enumerate(both):
            high = values.astype(jnp.bfloat16)
            table[device, 0, :, k * cells : (k + 1) * cells] = high
            low = (values - high.astype(jnp.float32)).astype(jnp.bfloat16)
            table[device, 1, :, k * cells : (k + 1) * cells] = low
    out_ref[...] = sum_plane(table, data)


def first_plane(info, sources, base, turns, block):
    span, cells = sources[0].shape
    modes = base.shape[0]
    return pl.pallas_call(
        functools.partial(first_plane_kernel, block),
        out_shape=[
            jax.ShapeDtypeStruct((modes, span), jnp.float32),
            jax.ShapeDtypeStruct((4, 2, modes, 2 * cells), jnp.bfloat16),
        ],
        in_specs=[IN_SMEM] + [IN_VMEM] * 6,
        out_specs=[IN_VMEM] * 2,
        scratch_shapes=[pltpu.VMEM((4, span, 2 * cells), jnp.bfloat16)],
        compiler_params=params(24),
        cost_estimate=pl.CostEstimate(
            flops=32 * cells * span * modes, bytes_accessed=4 * base.size, transcendentals=0
        ),
        name="first_plane",
    )(info, *resident(base, turns), *sources)


def tail_parts(rows):
    return next(k for k in (3, 2, 1) if rows % (8 * k) == 0)


def second_plane_kernel(groups, rows, block, info_ref, table_ref, other_ref, *refs):
    sources, outs, (sums, data) = refs[:4], refs[4 : 4 + groups], refs[4 + groups :]
    place_cells(info_ref, sources, block, data)
    sums[...] = sum_plane(table_ref, data)
    over = sums.shape[1] - LANES
    room = LANES - over
    parts = tail_parts(rows)
    step = rows // parts
    for r in range(groups):
        owner = jnp.bitwise_xor(info_ref[0], r)
        own = pl.ds(pl.multiple_of(owner * rows, 8), rows)
        first, second = other_ref[own], sums[own]
        mixed = jnp.concatenate([first[:, LANES:], second[:, LANES : LANES + room]], 1)
        tail = second[:, LANES + room :]
        tail = [tail[k * step : (k + 1) * step] for k in range(parts)]
        rest = LANES - parts * (over - room)
        tail = jnp.concatenate(tail + [jnp.zeros((step, rest), jnp.float32)], 1)
        whole = jnp.concatenate([first[:, :LANES], second[:, :LANES], mixed, tail], 0)
        outs[r][...] = whole.astype(jnp.bfloat16)


def second_plane(info, sources, table, other, groups, rows, block):
    span, cells = sources[0].shape
    modes = table.shape[2]
    chunk = jax.ShapeDtypeStruct((3 * rows + rows // tail_parts(rows), LANES), jnp.bfloat16)
    return pl.pallas_call(
        functools.partial(second_plane_kernel, groups, rows, block),
        out_shape=[chunk] * groups,
        in_specs=[IN_SMEM] + [IN_VMEM] * 6,
        out_specs=[IN_VMEM] * groups,
        scratch_shapes=[
            pltpu.VMEM((modes, span), jnp.float32),
            pltpu.VMEM((4, span, 2 * cells), jnp.bfloat16),
        ],
        compiler_params=params(24),
        cost_estimate=pl.CostEstimate(
            flops=32 * cells * span * modes, bytes_accessed=2 * table.size, transcendentals=0
        ),
        name="second_plane",
    )(info, *resident(table), other, *sources)


def mix_kernel(groups, groups_y, over, scale, info_ref, *refs):
    (scale_ref, regroup_ref), consts, refs = refs[:2], refs[2:5], refs[5:]
    chunks, mode_ref, outs, held = refs[:groups], refs[groups], refs[groups + 1 : -1], refs[-1]
    rows = held.shape[2]
    parts = tail_parts(rows)
    room = LANES - over
    left = over - room
    for t in range(4):
        place = jnp.bitwise_xor(info_ref[1], t)
        mine = [c for r, c in enumerate(chunks) if quad_of(r, groups_y) == t]
        total = mine[0][...].astype(jnp.float32)
        for ref in mine[1:]:
            total = total + ref[...].astype(jnp.float32)
        mixed, tail = total[2 * rows : 3 * rows], total[3 * rows :]
        tail = jnp.concatenate([tail[:, k * left : (k + 1) * left] for k in range(parts)], 0)
        zeros = jnp.zeros((rows, room), jnp.float32)
        held[place, 0] = total[:rows]
        held[place, 1] = jnp.concatenate([mixed[:, :over], zeros], 1)
        held[place, 2] = total[rows : 2 * rows]
        held[place, 3] = jnp.concatenate([mixed[:, over:], tail, zeros], 1)
    tiles = outs[0].shape[0] - 2
    for j in range(2):
        values = jnp.concatenate([held[g, j] for g in range(4)], 1) * scale_ref[j : j + 1]
        sums = jnp.dot(
            values.astype(jnp.bfloat16), regroup_ref[...], preferred_element_type=jnp.float32
        ).astype(jnp.bfloat16)
        for k in range(4):
            if j * 4 + k < tiles:
                for out in outs:
                    out[j * 4 + k] = sums[:, k * LANES : (k + 1) * LANES]
    for r, out in enumerate(outs):
        for j in range(2):
            value = held[jnp.bitwise_xor(info_ref[4], r), 2 + j] * scale
            out[tiles + j] = value.astype(jnp.bfloat16)
    mode_gradients(*consts, outs[0], mode_ref)


def packed_rows(tiles, rows, used):
    top = -(-rows // 16) * 8 if 2 * used <= LANES else rows
    return top, (tiles - 1) * rows + top


def mode_gradients(spread_ref, gather_ref, w_ref, s_ref, out_ref):
    tiles, rows = s_ref.shape[0] - 2, s_ref.shape[1]
    last, _, _, width = w_ref.shape
    half = spread_ref.shape[1] // (2 * LANES)
    for tile in range(tiles):
        wide = jnp.dot(s_ref[tile], spread_ref[...], preferred_element_type=jnp.float32)
        products = []
        for h in range(half):
            kz = tile * half + h
            if kz >= last:
                continue
            out_re = wide[:, (2 * h) * LANES : (2 * h + 1) * LANES]
            out_im = wide[:, (2 * h + 1) * LANES : (2 * h + 2) * LANES]
            real, imag = [], []
            for k in range(width // LANES):
                lane = slice(k * LANES, (k + 1) * LANES)
                w_re = w_ref[kz, 0, :, lane].astype(jnp.float32)
                w_im = w_ref[kz, 1, :, lane].astype(jnp.float32)
                real.append((w_re * out_re + w_im * out_im).astype(jnp.bfloat16))
                imag.append((w_re * out_im - w_im * out_re).astype(jnp.bfloat16))
            products += [jnp.concatenate(real, 1), jnp.concatenate(imag, 1)]
        sums = jnp.dot(
            jnp.concatenate(products, 0), gather_ref[...], preferred_element_type=jnp.float32
        )
        which = lax.broadcasted_iota(jnp.int32, (rows, LANES), 1) // (LANES // (2 * half))
        out = sums[:rows]
        for k in range(1, len(products)):
            out = jnp.where(which == k, sums[k * rows : (k + 1) * rows], out)
        out = jnp.where(which < len(products), out, 0.0)
        top = out_ref.shape[0] - (tiles - 1) * rows
        if tile == tiles - 1 and top < rows:
            lower = out[top:]
            if 2 * top > rows:
                zeros = jnp.zeros((2 * top - rows, LANES), jnp.float32)
                lower = jnp.concatenate([lower, zeros], 0)
            out = jnp.concatenate([out[:top, : LANES // 2], lower[:, : LANES // 2]], 1)
        out_ref[tile * rows : tile * rows + out.shape[0]] = out.astype(jnp.bfloat16)


def mix(info, chunks, scale, norm, regroup, spread, gather, weight, sizes):
    tiles, rows, over, scenes, groups_y = sizes
    half = spread.shape[1] // (2 * LANES)
    used = (MZ - (tiles - 1) * half) * spread.shape[0] // half
    out = jax.ShapeDtypeStruct((tiles + 2, rows, LANES), jnp.bfloat16)
    modes = jax.ShapeDtypeStruct((packed_rows(tiles, rows, used)[1], LANES), jnp.bfloat16)
    results = pl.pallas_call(
        functools.partial(mix_kernel, len(chunks), groups_y, over, norm),
        out_shape=[modes] + [out] * scenes,
        in_specs=[IN_SMEM] + [IN_VMEM] * (5 + len(chunks)),
        out_specs=[IN_VMEM] * (1 + scenes),
        scratch_shapes=[pltpu.VMEM((4, 4, rows, LANES), jnp.float32)],
        compiler_params=params(24),
        cost_estimate=pl.CostEstimate(
            flops=8 * tiles * rows * gather.size, bytes_accessed=2 * weight.size, transcendentals=0
        ),
        name="mix",
    )(info, *resident(scale, regroup, spread, gather, weight), *chunks)
    return results[0], results[1:]


def outer_kernel(scenes, spread_ref, pick_ref, *refs):
    spectra, out_ref = refs[:scenes], refs[scenes]
    rows = spectra[0].shape[1]
    copies = pick_ref.shape[2] // (2 * LANES)
    last = out_ref.shape[0] // (2 * copies * rows)
    wide = copies * LANES
    half = spread_ref.shape[1] // (2 * LANES)
    per_tile = pick_ref.shape[0]
    tiles = spectra[0].shape[0] - 2
    for kz in range(last):
        if kz % half == 0:
            grads = jnp.dot(
                jnp.concatenate([ref[kz // half] for ref in spectra], 0),
                spread_ref[...],
                preferred_element_type=jnp.float32,
            )
        if kz % per_tile == 0:
            field = jnp.concatenate([ref[tiles + kz // per_tile] for ref in spectra], 0)
        hats = jnp.dot(field, pick_ref[kz % per_tile], preferred_element_type=jnp.float32)
        lane = 2 * (kz % half) * LANES
        for k in range(wide // LANES):
            real, imag = 0.0, 0.0
            for s in range(scenes):
                here = slice(s * rows, (s + 1) * rows)
                hat_re = hats[here, k * LANES : (k + 1) * LANES]
                hat_im = hats[here, wide + k * LANES : wide + (k + 1) * LANES]
                out_re = grads[here, lane : lane + LANES]
                out_im = grads[here, lane + LANES : lane + 2 * LANES]
                real += out_re * hat_re + out_im * hat_im
                imag += out_im * hat_re - out_re * hat_im
            for part, value in enumerate((real, imag)):
                first = (kz * copies + k) * 2 + part
                out_ref[pl.ds(first, rows, stride=2 * copies * last), :] = value


def outer(spectra, spread, pick):
    tiles, rows, _ = spectra[0].shape
    wide = pick.shape[2] // 2
    return pl.pallas_call(
        functools.partial(outer_kernel, len(spectra)),
        out_shape=jax.ShapeDtypeStruct((rows * MZ * wide // LANES * 2, LANES), jnp.float32),
        in_specs=[IN_VMEM] * (2 + len(spectra)),
        out_specs=IN_VMEM,
        compiler_params=params(16),
        cost_estimate=pl.CostEstimate(
            flops=2 * tiles * rows * 4 * LANES * 12 * LANES,
            bytes_accessed=16 * tiles * rows * wide + 8 * tiles * rows * LANES * len(spectra),
            transcendentals=0,
        ),
        name="outer",
    )(*resident(spread, pick), *spectra)


def local_kernel(row_ref, column_ref, point_ref, grad_ref, out_ref, mixing):
    channels, cells_x, cells_y, length = grad_ref.shape
    picked = lax.dot_general(row_ref[...], point_ref[...], NT, preferred_element_type=jnp.float32)
    spread = jnp.dot(
        picked.astype(jnp.bfloat16), column_ref[...], preferred_element_type=jnp.float32
    )
    row = lax.broadcasted_iota(jnp.int32, spread.shape, 0) % cells_y
    column = lax.broadcasted_iota(jnp.int32, spread.shape, 1) % cells_y
    mixing[...] = jnp.where(row == column, spread, 0.0).astype(jnp.bfloat16)

    @pl.loop(0, cells_x, step=4)
    def _(start):
        for x in range(4):
            out_ref[start + x] = jnp.dot(
                mixing[...],
                grad_ref[:, start + x].reshape(channels * cells_y, length),
                preferred_element_type=jnp.float32,
            ).astype(out_ref.dtype)


def local(cell_rows, cell_columns, point, grad):
    channels, cells_x, cells_y, length = grad.shape
    width = channels * cells_y
    return pl.pallas_call(
        local_kernel,
        out_shape=jax.ShapeDtypeStruct((cells_x, width, length), jnp.bfloat16),
        in_specs=[IN_VMEM] * 4,
        out_specs=IN_VMEM,
        scratch_shapes=[pltpu.VMEM((width, width), jnp.bfloat16)],
        compiler_params=params(16),
        cost_estimate=pl.CostEstimate(
            flops=2 * grad.size * width, bytes_accessed=4 * grad.size, transcendentals=0
        ),
        name="local",
    )(*resident(cell_rows, cell_columns, point, grad))


def inverse_kernel(groups, per_tile, here, info_ref, t_ref, order_ref, z_ref, local_ref, *refs):
    chunks, (out_ref, modes, held, built, sems) = refs[:groups], refs[groups:]
    channels, cells_x, cells_y, length = built.shape
    rows = modes.shape[0] // groups
    tiles = channels // per_tile
    last = modes.shape[1] // LANES - 1
    top = chunks[0].shape[0] - last * rows
    for r in range(groups):
        own = pl.ds(pl.multiple_of(jnp.bitwise_xor(info_ref[0], r) * rows, 8), rows)
        for j in range(last):
            value = chunks[r][j * rows : (j + 1) * rows]
            modes[own, j * LANES : (j + 1) * LANES] = value.astype(jnp.float32)
        value = chunks[r][last * rows :].astype(jnp.float32)
        if top < rows:
            middle = LANES // 2
            value = jnp.concatenate([value[:, :middle], value[: rows - top, middle:]], 0)
            value = jnp.concatenate([value, jnp.zeros_like(value)], 1)
        modes[own, last * LANES :] = value
    sums = jnp.dot(
        t_ref[info_ref[3]], modes[...].astype(jnp.bfloat16), preferred_element_type=jnp.float32
    )
    cells = sums.shape[0] // 2
    cosine, sine = sums[:cells], sums[cells:]
    wide = sine.shape[1]
    lane = lax.broadcasted_iota(jnp.int32, sine.shape, 1)
    first = lane % (2 * channels) < channels
    turned = jnp.where(
        first, -pltpu.roll(sine, wide - channels, 1), pltpu.roll(sine, channels, 1)
    )
    back = (cosine + turned).astype(jnp.bfloat16)
    ordered = jnp.dot(back, order_ref[...], preferred_element_type=jnp.float32)
    held[...] = ordered.astype(jnp.bfloat16).reshape(held.shape)

    span = tiles * cells_y
    copies = []
    for start in range(0, cells_x, here):
        stack = []
        for x in range(start, start + here):
            back = held[x]
            stack += [back[:, k * LANES : (k + 1) * LANES] for k in range(tiles)]
        stack = jnp.concatenate(stack, 0)
        spectral = jnp.dot(
            jnp.concatenate([stack, stack], 1), z_ref[...], preferred_element_type=jnp.float32
        )
        for x in range(here):
            for j in range(per_tile):
                both = (
                    spectral[x * span : (x + 1) * span, j * length : (j + 1) * length]
                    + local_ref[start + x, j * span : (j + 1) * span].astype(jnp.float32)
                ).astype(jnp.bfloat16)
                for k in range(tiles):
                    built[k * per_tile + j, start + x] = both[k * cells_y : (k + 1) * cells_y]
        copies.append(
            pltpu.make_async_copy(
                built.at[:, pl.ds(start, here)],
                out_ref.at[:, pl.ds(start, here)],
                sems.at[start // here],
            )
        )
        copies[-1].start()
    for copy in copies:
        copy.wait()


def inverse(info, chunks, table, order, z_table, local_part, shape, per_tile, here):
    channels, cells_x, cells_y, length = shape
    return pl.pallas_call(
        functools.partial(inverse_kernel, len(chunks), per_tile, here),
        out_shape=jax.ShapeDtypeStruct(shape, jnp.bfloat16),
        in_specs=[IN_SMEM] + [IN_VMEM] * (4 + len(chunks)),
        out_specs=IN_HBM,
        scratch_shapes=[
            pltpu.VMEM((table.shape[2], order.shape[0]), jnp.float32),
            pltpu.VMEM((cells_x, cells_y, order.shape[1]), jnp.bfloat16),
            pltpu.VMEM(shape, jnp.bfloat16),
            pltpu.SemaphoreType.DMA((cells_x // here,)),
        ],
        compiler_params=params(28),
        cost_estimate=pl.CostEstimate(
            flops=2 * local_part.size * LANES, bytes_accessed=4 * local_part.size, transcendentals=0
        ),
        name="inverse",
    )(info, *resident(table, order, z_table, local_part), *chunks)


def flip(value, axes, size, r):
    return lax.ppermute(value, axes, [(i, i ^ r) for i in range(size)])


def body(field_in, grad_pre, spec_weight, point_weight):
    _, channels, cells_x, cells_y, cells_z = field_in.shape
    groups_x, groups_y = lax.axis_size("gx"), lax.axis_size("gy")
    groups, scenes = groups_x * groups_y, lax.axis_size("scene")
    group_axes = ("gx", "gy")
    total_x, total_y = cells_x * groups_x, cells_y * groups_y
    cells = cells_x * cells_y
    norm = float(total_x * total_y * cells_z) ** -0.5
    modes_xd, modes_yd = spec_weight.shape[:2]
    modes = modes_xd * modes_yd
    rows = -(-modes // 8) * 8
    half = LANES // (2 * channels)
    tiles = -(-MZ // half)
    block = channels // 4
    slot = 16
    per_tile = LANES // (2 * slot)
    sizes = (groups, groups_y, modes_xd, modes_yd, total_x, total_y)

    me = lax.axis_index(group_axes)
    at_x, at_y = lax.axis_index("gx"), lax.axis_index("gy")
    quad = at_x % 2 * 2 + at_y % 2
    base, turns = (jnp.asarray(t) for t in forward_table(rows, sizes, cells_x, cells_y))
    if groups * groups * rows * 2 * cells <= 1 << 24:
        inverse_t = jnp.asarray(
            np.stack([inverse_table(np, i, rows, sizes, cells_x, cells_y) for i in range(groups)])
        )
        inverse_at = me
    else:
        inverse_t = inverse_table(jnp, me, rows, sizes, cells_x, cells_y)[None]
        inverse_at = 0 * me
    forward_at = at_x // 2 * (groups_y // 2) + at_y // 2
    info = jnp.stack([me, quad, forward_at, inverse_at, lax.axis_index("scene")])

    regroup = jnp.asarray(regroup_table(channels, block, half))
    inverse_z = jnp.asarray(inverse_z_table(cells_z, per_tile, slot, norm))
    order = jnp.asarray(order_table(channels, tiles * half, per_tile, slot))
    lane = np.arange(LANES)
    spread = jnp.asarray(spread_table(channels, half, lane % channels))
    gather = jnp.asarray(gather_table(channels, LANES // channels))
    here = channels // scenes
    pair = np.arange(here * channels)
    kz_tile = LANES // (2 * block)
    pick = spread_table(here, kz_tile, pair // channels).reshape(LANES, kz_tile, -1)
    pick = jnp.asarray(pick.transpose(1, 0, 2))
    cell_rows, cell_columns = (jnp.asarray(t) for t in cell_tables(channels, per_tile, cells_y))
    scale = np.full((2, 4, kz_tile, 2 * block), 2.0 * norm, np.float32)
    scale[0, :, 0] = norm
    scale = jnp.asarray(scale.reshape(2, 4 * LANES))

    def cells_of(field):
        mine = along_z(info, field.reshape(channels, cells, cells_z), block)
        return [mine[0]] + [
            flip(mine[t], group_axes, groups, quad_offset(t, groups_y)) for t in range(1, 4)
        ]

    grad_cells = cells_of(grad_pre)
    field, _ = lax.optimization_barrier((field_in, grad_cells[0]))
    field_cells = cells_of(field)
    grad_sums, table = first_plane(info, grad_cells, base, turns, block)
    sums = second_plane(info, field_cells, table, grad_sums, groups, rows, block)
    got = {0: sums[0], 1: flip(sums[1], group_axes, groups, 1)}
    far = [r for r in range(groups - 1, 1, -1) if r % groups_y >= groups_y // 2]
    for r in far:
        got[r] = flip(sums[r], group_axes, groups, r)
    near = [r for r in range(2, groups) if r not in far]
    waiting, _ = lax.optimization_barrier(([sums[r] for r in near], got[1]))
    for r, value in zip(near, waiting):
        got[r] = flip(value, group_axes, groups, r)
    got = [got[r] for r in range(groups)]
    weight = spec_weight.reshape(modes, MZ, 2, channels * channels)
    weight = jnp.pad(weight.transpose(1, 2, 0, 3), ((0, 0), (0, 0), (0, rows - modes), (0, 0)))
    local_part = local(
        cell_rows,
        cell_columns,
        point_weight,
        grad_pre.reshape(channels, cells_x, cells_y, cells_z),
    )
    got, weight, local_part = lax.optimization_barrier((got, weight, local_part))
    over = 2 * MZ * block - LANES
    mode_grad, spectra = mix(
        info,
        got,
        scale,
        norm,
        regroup,
        spread,
        gather,
        weight,
        (tiles, rows, over, scenes, groups_y),
    )

    along_y = [mode_grad] + [None] * (groups_y - 1)
    for r in range(groups_y - 1, 0, -1):
        along_y[r] = flip(mode_grad, "gy", groups_y, r)
    gathered = list(along_y)
    for r in range(1, groups_x):
        gathered += [flip(value, "gx", groups_x, r) for value in along_y]

    got, before = [spectra[0]], ()
    for r in range(1, scenes):
        value, before = lax.optimization_barrier((spectra[r], along_y[-1]))
        got.append(flip(value, "scene", scenes, r))
    spectra = got
    grad_field = inverse(
        info,
        gathered,
        inverse_t,
        order,
        inverse_z,
        local_part,
        (channels, cells_x, cells_y, cells_z),
        per_tile,
        2,
    )
    spectra, grad_field = lax.optimization_barrier((spectra, grad_field))
    grads = outer(spectra, spread, pick)
    grads = grads.reshape(rows, MZ, here * channels // LANES, 2, LANES)[:modes]
    grad_spec = grads.transpose(0, 1, 3, 2, 4).reshape(
        modes_xd, modes_yd, MZ, 2, here * channels
    )

    return grad_field[None], grad_spec


def solution(mesh):
    return jax.shard_map(
        body,
        mesh=mesh,
        in_specs=(
            P("scene", None, "gx", "gy", None),
            P("scene", None, "gx", "gy", None),
            P("gx", "gy", None, None, None),
            P(),
        ),
        out_specs=(P("scene", None, "gx", "gy", None), P("gx", "gy", None, None, "scene")),
        check_vma=False,
    )
```

```python
import functools
import math

import jax
import jax.numpy as jnp
import ml_dtypes
import numpy as np
from jax import lax
from jax.experimental import pallas as pl
from jax.experimental.pallas import tpu as pltpu
from jax.sharding import PartitionSpec as P

MX = 24
MY = 24
MZ = 13
LANES = 128
NT = (((1,), (1,)), ((), ()))
BF16 = ml_dtypes.bfloat16


def angles(xp, index, modes, positions, length):
    freq = xp.where(index < modes // 2, index, index - modes)
    turns = (freq[..., None] * positions) % length
    return turns.astype(np.float32) * np.float32(2.0 * math.pi / length)


def mode_angles(xp, rows, sizes, local_x, local_y):
    groups, groups_y, modes_xd, modes_yd, total_x, total_y = sizes
    owner = xp.repeat(xp.arange(groups, dtype=np.int32), rows)
    within = xp.tile(xp.arange(rows, dtype=np.int32), groups)
    kx = owner // groups_y * modes_xd + xp.minimum(within // modes_yd, modes_xd - 1)
    ky = owner % groups_y * modes_yd + within % modes_yd
    angle_x = angles(xp, kx, MX, local_x, total_x)
    angle_y = angles(xp, ky, MY, local_y, total_y)
    theta = (angle_x[:, :, None] + angle_y[:, None, :]).reshape(owner.shape[0], -1)
    return theta, (within < modes_xd * modes_yd)[:, None]


def device_cells(xp, me, groups_y, cells_x, cells_y):
    local_x = me // groups_y * cells_x + xp.arange(cells_x, dtype=np.int32)
    local_y = me % groups_y * cells_y + xp.arange(cells_y, dtype=np.int32)
    return local_x, local_y


def forward_table(rows, sizes, cells_x, cells_y):
    groups, groups_y = sizes[:2]
    theta, real = mode_angles(
        np, rows, sizes, *device_cells(np, np.int32(0), groups_y, cells_x, cells_y)
    )
    base = np.where(real, np.concatenate([np.cos(theta), np.sin(theta)], 1), np.float32(0))
    turns = []
    for x in range(0, groups // groups_y, 2):
        for y in range(0, groups_y, 2):
            turn = np.zeros((groups * rows, LANES), np.float32)
            for t in range(4):
                device = np.int32(x * groups_y + y + quad_offset(t, groups_y))
                local_x, local_y = device_cells(np, device, groups_y, cells_x, cells_y)
                angle, _ = mode_angles(np, rows, sizes, local_x[:1], local_y[:1])
                turn[:, 2 * t] = np.cos(angle[:, 0])
                turn[:, 2 * t + 1] = np.sin(angle[:, 0])
            turns.append(turn)
    return base, np.stack(turns)


def inverse_table(xp, me, rows, sizes, cells_x, cells_y):
    theta, real = mode_angles(
        xp, rows, sizes, *device_cells(xp, me, sizes[1], cells_x, cells_y)
    )
    cosine = xp.where(real, xp.cos(theta), np.float32(0))
    sine = xp.where(real, xp.sin(theta), np.float32(0))
    return xp.concatenate([cosine.T, sine.T], 0).astype(BF16)


def quad_offset(t, groups_y):
    return t // 2 * groups_y + t % 2


def quad_of(r, groups_y):
    return r // groups_y % 2 * 2 + r % groups_y % 2


def split16(values):
    high = values.astype(BF16)
    low = (values - high.astype(np.float32)).astype(BF16)
    return high, low


def inverse_z_table(length, per_tile, slot, norm):
    modes, cells = np.arange(MZ, dtype=np.int32), np.arange(length, dtype=np.int32)
    theta = angles(np, modes, 2 * MZ, cells, length)
    parts = np.stack([np.cos(theta), -np.sin(theta)], 0) * np.float32(norm)
    table = np.zeros((per_tile, 2, slot, per_tile, length), np.float32)
    for c in range(per_tile):
        table[c, :, :MZ, c] = parts
    high, low = split16(table.reshape(LANES, per_tile * length))
    return np.concatenate([high, low], 0)


def order_table(channels, kz_pad, per_tile, slot):
    table = np.zeros((kz_pad, 2, channels, channels // per_tile, per_tile, 2, slot), np.float32)
    for kz in range(MZ):
        for part in range(2):
            for c in range(channels):
                table[kz, part, c, c // per_tile, c % per_tile, part, kz] = 1
    return table.reshape(kz_pad * 2 * channels, -1).astype(BF16)


def spread_table(channels, half, copies):
    table = np.zeros((half, 2, channels, half, 2, copies.shape[0]), np.float32)
    for h in range(half):
        for part in range(2):
            table[h, part, copies, h, part, np.arange(copies.shape[0])] = 1
    return table.reshape(half * 2 * channels, -1).astype(BF16)


def gather_table(channels, copies):
    table = np.zeros((channels, channels, copies, channels), np.float32)
    for i in range(channels):
        table[i, :, :, i] = 1
    return table.reshape(channels * channels, -1).astype(BF16)


def cell_tables(channels, per_tile, cells_y):
    rows = np.zeros((per_tile, channels // per_tile, cells_y, channels), np.float32)
    for c in range(channels):
        rows[c % per_tile, c // per_tile, :, c] = 1
    columns = np.repeat(np.eye(channels, dtype=np.float32), cells_y, 1)
    return rows.reshape(-1, channels).astype(BF16), columns.astype(BF16)


def regroup_table(channels, block, half):
    groups = channels // block
    kz_tile = LANES // (2 * block)
    table = np.zeros((groups, kz_tile, 2, block, kz_tile // half, half, 2, groups, block), np.float32)
    for g in range(groups):
        for kz in range(kz_tile):
            for part in range(2):
                for c in range(block):
                    table[g, kz, part, c, kz // half, kz % half, part, g, c] = 1
    return table.reshape(groups * LANES, -1).astype(BF16)


def params(mib):
    return pltpu.CompilerParams(vmem_limit_bytes=mib * 1024 * 1024)


IN_VMEM = pl.BlockSpec(memory_space=pltpu.VMEM)
IN_SMEM = pl.BlockSpec(memory_space=pltpu.SMEM)
IN_HBM = pl.BlockSpec(memory_space=pl.ANY)


def resident(*arrays):
    return [pltpu.with_memory_space_constraint(a, pltpu.VMEM) for a in arrays]


def along_z_kernel(info_ref, x_ref, *rest):
    outs, table = rest[:4], rest[4]
    block, span, length = table.shape
    padded = -(-2 * MZ // 16) * 16
    row = lax.broadcasted_iota(jnp.int32, (padded, length), 0)
    cell = lax.broadcasted_iota(jnp.int32, (padded, length), 1)
    theta = ((row // 2 * cell) % length).astype(jnp.float32) * (2.0 * math.pi / length)
    parts = jnp.where(row % 2 == 0, jnp.cos(theta), -jnp.sin(theta))
    row = lax.broadcasted_iota(jnp.int32, (span, padded), 0) // block
    repeat = (row == lax.broadcasted_iota(jnp.int32, (span, padded), 1)).astype(jnp.bfloat16)
    rows = jnp.dot(repeat, parts.astype(jnp.bfloat16), preferred_element_type=jnp.float32)
    channel = lax.broadcasted_iota(jnp.int32, rows.shape, 0) % block
    for c in range(block):
        table[c] = jnp.where(channel == c, rows, 0.0).astype(jnp.bfloat16)
    for t in range(4):
        first = jnp.bitwise_xor(info_ref[1], t) * block
        total = None
        for c in range(block):
            term = lax.dot_general(
                table[c], x_ref[first + c], NT, preferred_element_type=jnp.float32
            )
            total = term if total is None else total + term
        outs[t][...] = total.astype(jnp.bfloat16)


def along_z(info, field, block):
    channels, cells, length = field.shape
    span = 2 * MZ * block
    return pl.pallas_call(
        along_z_kernel,
        out_shape=[jax.ShapeDtypeStruct((span, cells), jnp.bfloat16)] * 4,
        in_specs=[IN_SMEM, IN_VMEM],
        out_specs=[IN_VMEM] * 4,
        scratch_shapes=[pltpu.VMEM((block, span, length), jnp.bfloat16)],
        compiler_params=params(12),
        cost_estimate=pl.CostEstimate(
            flops=2 * span * cells * length * channels,
            bytes_accessed=2 * field.size,
            transcendentals=0,
        ),
        name="along_z",
    )(info, *resident(field))


def place_cells(info_ref, sources, block, data):
    span, cells = sources[0].shape
    for t in range(4):
        place = jnp.bitwise_xor(info_ref[1], t)
        value = sources[t][...].astype(jnp.float32)
        turned = []
        for k in range(0, span, 2 * block):
            turned += [value[k + block : k + 2 * block], -value[k : k + block]]
        data[place, :, :cells] = sources[t][...]
        data[place, :, cells:] = jnp.concatenate(turned, 0).astype(jnp.bfloat16)


def sum_plane(table, data):
    total = None
    for device in range(4):
        for part in range(2):
            term = lax.dot_general(
                table[device, part], data[device], NT, preferred_element_type=jnp.float32
            )
            total = term if total is None else total + term
    return total


def first_plane_kernel(block, info_ref, base_ref, turn_ref, *refs):
    sources, (out_ref, table, data) = refs[:4], refs[4:]
    cells = sources[0].shape[1]
    place_cells(info_ref, sources, block, data)
    turns = turn_ref[info_ref[2]]
    cosine, sine = base_ref[:, :cells], base_ref[:, cells:]
    for device in range(4):
        turn_cos = turns[:, 2 * device : 2 * device + 1]
        turn_sin = turns[:, 2 * device + 1 : 2 * device + 2]
        both = (cosine * turn_cos - sine * turn_sin, sine * turn_cos + cosine * turn_sin)
        for k, values in enumerate(both):
            high = values.astype(jnp.bfloat16)
            table[device, 0, :, k * cells : (k + 1) * cells] = high
            low = (values - high.astype(jnp.float32)).astype(jnp.bfloat16)
            table[device, 1, :, k * cells : (k + 1) * cells] = low
    out_ref[...] = sum_plane(table, data)


def first_plane(info, sources, base, turns, block):
    span, cells = sources[0].shape
    modes = base.shape[0]
    return pl.pallas_call(
        functools.partial(first_plane_kernel, block),
        out_shape=[
            jax.ShapeDtypeStruct((modes, span), jnp.float32),
            jax.ShapeDtypeStruct((4, 2, modes, 2 * cells), jnp.bfloat16),
        ],
        in_specs=[IN_SMEM] + [IN_VMEM] * 6,
        out_specs=[IN_VMEM] * 2,
        scratch_shapes=[pltpu.VMEM((4, span, 2 * cells), jnp.bfloat16)],
        compiler_params=params(24),
        cost_estimate=pl.CostEstimate(
            flops=32 * cells * span * modes, bytes_accessed=4 * base.size, transcendentals=0
        ),
        name="first_plane",
    )(info, *resident(base, turns), *sources)


def tail_parts(rows):
    return next(k for k in (3, 2, 1) if rows % (8 * k) == 0)


def second_plane_kernel(groups, rows, block, info_ref, table_ref, other_ref, *refs):
    sources, outs, (sums, data) = refs[:4], refs[4 : 4 + groups], refs[4 + groups :]
    place_cells(info_ref, sources, block, data)
    sums[...] = sum_plane(table_ref, data)
    over = sums.shape[1] - LANES
    room = LANES - over
    parts = tail_parts(rows)
    step = rows // parts
    for r in range(groups):
        owner = jnp.bitwise_xor(info_ref[0], r)
        own = pl.ds(pl.multiple_of(owner * rows, 8), rows)
        first, second = other_ref[own], sums[own]
        mixed = jnp.concatenate([first[:, LANES:], second[:, LANES : LANES + room]], 1)
        tail = second[:, LANES + room :]
        tail = [tail[k * step : (k + 1) * step] for k in range(parts)]
        rest = LANES - parts * (over - room)
        tail = jnp.concatenate(tail + [jnp.zeros((step, rest), jnp.float32)], 1)
        whole = jnp.concatenate([first[:, :LANES], second[:, :LANES], mixed, tail], 0)
        outs[r][...] = whole.astype(jnp.bfloat16)


def second_plane(info, sources, table, other, groups, rows, block):
    span, cells = sources[0].shape
    modes = table.shape[2]
    chunk = jax.ShapeDtypeStruct((3 * rows + rows // tail_parts(rows), LANES), jnp.bfloat16)
    return pl.pallas_call(
        functools.partial(second_plane_kernel, groups, rows, block),
        out_shape=[chunk] * groups,
        in_specs=[IN_SMEM] + [IN_VMEM] * 6,
        out_specs=[IN_VMEM] * groups,
        scratch_shapes=[
            pltpu.VMEM((modes, span), jnp.float32),
            pltpu.VMEM((4, span, 2 * cells), jnp.bfloat16),
        ],
        compiler_params=params(24),
        cost_estimate=pl.CostEstimate(
            flops=32 * cells * span * modes, bytes_accessed=2 * table.size, transcendentals=0
        ),
        name="second_plane",
    )(info, *resident(table), other, *sources)


def mix_kernel(groups, groups_y, over, scale, info_ref, *refs):
    (scale_ref, regroup_ref), consts, refs = refs[:2], refs[2:5], refs[5:]
    chunks, mode_ref, outs, held = refs[:groups], refs[groups], refs[groups + 1 : -1], refs[-1]
    rows = held.shape[2]
    parts = tail_parts(rows)
    room = LANES - over
    left = over - room
    for t in range(4):
        place = jnp.bitwise_xor(info_ref[1], t)
        mine = [c for r, c in enumerate(chunks) if quad_of(r, groups_y) == t]
        total = mine[0][...].astype(jnp.float32)
        for ref in mine[1:]:
            total = total + ref[...].astype(jnp.float32)
        mixed, tail = total[2 * rows : 3 * rows], total[3 * rows :]
        tail = jnp.concatenate([tail[:, k * left : (k + 1) * left] for k in range(parts)], 0)
        zeros = jnp.zeros((rows, room), jnp.float32)
        held[place, 0] = total[:rows]
        held[place, 1] = jnp.concatenate([mixed[:, :over], zeros], 1)
        held[place, 2] = total[rows : 2 * rows]
        held[place, 3] = jnp.concatenate([mixed[:, over:], tail, zeros], 1)
    tiles = outs[0].shape[0] - 2
    for j in range(2):
        values = jnp.concatenate([held[g, j] for g in range(4)], 1) * scale_ref[j : j + 1]
        sums = jnp.dot(
            values.astype(jnp.bfloat16), regroup_ref[...], preferred_element_type=jnp.float32
        ).astype(jnp.bfloat16)
        for k in range(4):
            if j * 4 + k < tiles:
                for out in outs:
                    out[j * 4 + k] = sums[:, k * LANES : (k + 1) * LANES]
    for r, out in enumerate(outs):
        for j in range(2):
            value = held[jnp.bitwise_xor(info_ref[4], r), 2 + j] * scale
            out[tiles + j] = value.astype(jnp.bfloat16)
    mode_gradients(*consts, outs[0], mode_ref)


def packed_rows(tiles, rows, used):
    top = -(-rows // 16) * 8 if 2 * used <= LANES else rows
    return top, (tiles - 1) * rows + top


def mode_gradients(spread_ref, gather_ref, w_ref, s_ref, out_ref):
    tiles, rows = s_ref.shape[0] - 2, s_ref.shape[1]
    last, _, _, width = w_ref.shape
    half = spread_ref.shape[1] // (2 * LANES)
    for tile in range(tiles):
        wide = jnp.dot(s_ref[tile], spread_ref[...], preferred_element_type=jnp.float32)
        products = []
        for h in range(half):
            kz = tile * half + h
            if kz >= last:
                continue
            out_re = wide[:, (2 * h) * LANES : (2 * h + 1) * LANES]
            out_im = wide[:, (2 * h + 1) * LANES : (2 * h + 2) * LANES]
            real, imag = [], []
            for k in range(width // LANES):
                lane = slice(k * LANES, (k + 1) * LANES)
                w_re = w_ref[kz, 0, :, lane].astype(jnp.float32)
                w_im = w_ref[kz, 1, :, lane].astype(jnp.float32)
                real.append((w_re * out_re + w_im * out_im).astype(jnp.bfloat16))
                imag.append((w_re * out_im - w_im * out_re).astype(jnp.bfloat16))
            products += [jnp.concatenate(real, 1), jnp.concatenate(imag, 1)]
        sums = jnp.dot(
            jnp.concatenate(products, 0), gather_ref[...], preferred_element_type=jnp.float32
        )
        which = lax.broadcasted_iota(jnp.int32, (rows, LANES), 1) // (LANES // (2 * half))
        out = sums[:rows]
        for k in range(1, len(products)):
            out = jnp.where(which == k, sums[k * rows : (k + 1) * rows], out)
        out = jnp.where(which < len(products), out, 0.0)
        top = out_ref.shape[0] - (tiles - 1) * rows
        if tile == tiles - 1 and top < rows:
            lower = out[top:]
            if 2 * top > rows:
                zeros = jnp.zeros((2 * top - rows, LANES), jnp.float32)
                lower = jnp.concatenate([lower, zeros], 0)
            out = jnp.concatenate([out[:top, : LANES // 2], lower[:, : LANES // 2]], 1)
        out_ref[tile * rows : tile * rows + out.shape[0]] = out.astype(jnp.bfloat16)


def mix(info, chunks, scale, norm, regroup, spread, gather, weight, sizes):
    tiles, rows, over, scenes, groups_y = sizes
    half = spread.shape[1] // (2 * LANES)
    used = (MZ - (tiles - 1) * half) * spread.shape[0] // half
    out = jax.ShapeDtypeStruct((tiles + 2, rows, LANES), jnp.bfloat16)
    modes = jax.ShapeDtypeStruct((packed_rows(tiles, rows, used)[1], LANES), jnp.bfloat16)
    results = pl.pallas_call(
        functools.partial(mix_kernel, len(chunks), groups_y, over, norm),
        out_shape=[modes] + [out] * scenes,
        in_specs=[IN_SMEM] + [IN_VMEM] * (5 + len(chunks)),
        out_specs=[IN_VMEM] * (1 + scenes),
        scratch_shapes=[pltpu.VMEM((4, 4, rows, LANES), jnp.float32)],
        compiler_params=params(24),
        cost_estimate=pl.CostEstimate(
            flops=8 * tiles * rows * gather.size, bytes_accessed=2 * weight.size, transcendentals=0
        ),
        name="mix",
    )(info, *resident(scale, regroup, spread, gather, weight), *chunks)
    return results[0], results[1:]


def outer_kernel(scenes, spread_ref, pick_ref, *refs):
    spectra, out_ref = refs[:scenes], refs[scenes]
    rows = spectra[0].shape[1]
    copies = pick_ref.shape[2] // (2 * LANES)
    last = out_ref.shape[0] // (2 * copies * rows)
    wide = copies * LANES
    half = spread_ref.shape[1] // (2 * LANES)
    per_tile = pick_ref.shape[0]
    tiles = spectra[0].shape[0] - 2
    for kz in range(last):
        if kz % half == 0:
            grads = jnp.dot(
                jnp.concatenate([ref[kz // half] for ref in spectra], 0),
                spread_ref[...],
                preferred_element_type=jnp.float32,
            )
        if kz % per_tile == 0:
            field = jnp.concatenate([ref[tiles + kz // per_tile] for ref in spectra], 0)
        hats = jnp.dot(field, pick_ref[kz % per_tile], preferred_element_type=jnp.float32)
        lane = 2 * (kz % half) * LANES
        for k in range(wide // LANES):
            real, imag = 0.0, 0.0
            for s in range(scenes):
                here = slice(s * rows, (s + 1) * rows)
                hat_re = hats[here, k * LANES : (k + 1) * LANES]
                hat_im = hats[here, wide + k * LANES : wide + (k + 1) * LANES]
                out_re = grads[here, lane : lane + LANES]
                out_im = grads[here, lane + LANES : lane + 2 * LANES]
                real += out_re * hat_re + out_im * hat_im
                imag += out_im * hat_re - out_re * hat_im
            for part, value in enumerate((real, imag)):
                first = (kz * copies + k) * 2 + part
                out_ref[pl.ds(first, rows, stride=2 * copies * last), :] = value


def outer(spectra, spread, pick):
    tiles, rows, _ = spectra[0].shape
    wide = pick.shape[2] // 2
    return pl.pallas_call(
        functools.partial(outer_kernel, len(spectra)),
        out_shape=jax.ShapeDtypeStruct((rows * MZ * wide // LANES * 2, LANES), jnp.float32),
        in_specs=[IN_VMEM] * (2 + len(spectra)),
        out_specs=IN_VMEM,
        compiler_params=params(16),
        cost_estimate=pl.CostEstimate(
            flops=2 * tiles * rows * 4 * LANES * 12 * LANES,
            bytes_accessed=16 * tiles * rows * wide + 8 * tiles * rows * LANES * len(spectra),
            transcendentals=0,
        ),
        name="outer",
    )(*resident(spread, pick), *spectra)


def local_kernel(row_ref, column_ref, point_ref, grad_ref, out_ref, mixing):
    channels, cells_x, cells_y, length = grad_ref.shape
    picked = lax.dot_general(row_ref[...], point_ref[...], NT, preferred_element_type=jnp.float32)
    spread = jnp.dot(
        picked.astype(jnp.bfloat16), column_ref[...], preferred_element_type=jnp.float32
    )
    row = lax.broadcasted_iota(jnp.int32, spread.shape, 0) % cells_y
    column = lax.broadcasted_iota(jnp.int32, spread.shape, 1) % cells_y
    mixing[...] = jnp.where(row == column, spread, 0.0).astype(jnp.bfloat16)

    @pl.loop(0, cells_x, step=4)
    def _(start):
        for x in range(4):
            out_ref[start + x] = jnp.dot(
                mixing[...],
                grad_ref[:, start + x].reshape(channels * cells_y, length),
                preferred_element_type=jnp.float32,
            ).astype(out_ref.dtype)


def local(cell_rows, cell_columns, point, grad):
    channels, cells_x, cells_y, length = grad.shape
    width = channels * cells_y
    return pl.pallas_call(
        local_kernel,
        out_shape=jax.ShapeDtypeStruct((cells_x, width, length), jnp.bfloat16),
        in_specs=[IN_VMEM] * 4,
        out_specs=IN_VMEM,
        scratch_shapes=[pltpu.VMEM((width, width), jnp.bfloat16)],
        compiler_params=params(16),
        cost_estimate=pl.CostEstimate(
            flops=2 * grad.size * width, bytes_accessed=4 * grad.size, transcendentals=0
        ),
        name="local",
    )(*resident(cell_rows, cell_columns, point, grad))


def inverse_kernel(groups, per_tile, here, info_ref, t_ref, order_ref, z_ref, local_ref, *refs):
    chunks, (out_ref, modes, held, built, sems) = refs[:groups], refs[groups:]
    channels, cells_x, cells_y, length = built.shape
    rows = modes.shape[0] // groups
    tiles = channels // per_tile
    last = modes.shape[1] // LANES - 1
    top = chunks[0].shape[0] - last * rows
    for r in range(groups):
        own = pl.ds(pl.multiple_of(jnp.bitwise_xor(info_ref[0], r) * rows, 8), rows)
        for j in range(last):
            value = chunks[r][j * rows : (j + 1) * rows]
            modes[own, j * LANES : (j + 1) * LANES] = value.astype(jnp.float32)
        value = chunks[r][last * rows :].astype(jnp.float32)
        if top < rows:
            middle = LANES // 2
            value = jnp.concatenate([value[:, :middle], value[: rows - top, middle:]], 0)
            value = jnp.concatenate([value, jnp.zeros_like(value)], 1)
        modes[own, last * LANES :] = value
    sums = jnp.dot(
        t_ref[info_ref[3]], modes[...].astype(jnp.bfloat16), preferred_element_type=jnp.float32
    )
    cells = sums.shape[0] // 2
    cosine, sine = sums[:cells], sums[cells:]
    wide = sine.shape[1]
    lane = lax.broadcasted_iota(jnp.int32, sine.shape, 1)
    first = lane % (2 * channels) < channels
    turned = jnp.where(
        first, -pltpu.roll(sine, wide - channels, 1), pltpu.roll(sine, channels, 1)
    )
    back = (cosine + turned).astype(jnp.bfloat16)
    ordered = jnp.dot(back, order_ref[...], preferred_element_type=jnp.float32)
    held[...] = ordered.astype(jnp.bfloat16).reshape(held.shape)

    span = tiles * cells_y
    copies = []
    for start in range(0, cells_x, here):
        stack = []
        for x in range(start, start + here):
            back = held[x]
            stack += [back[:, k * LANES : (k + 1) * LANES] for k in range(tiles)]
        stack = jnp.concatenate(stack, 0)
        spectral = jnp.dot(
            jnp.concatenate([stack, stack], 1), z_ref[...], preferred_element_type=jnp.float32
        )
        for x in range(here):
            for j in range(per_tile):
                both = (
                    spectral[x * span : (x + 1) * span, j * length : (j + 1) * length]
                    + local_ref[start + x, j * span : (j + 1) * span].astype(jnp.float32)
                ).astype(jnp.bfloat16)
                for k in range(tiles):
                    built[k * per_tile + j, start + x] = both[k * cells_y : (k + 1) * cells_y]
        copies.append(
            pltpu.make_async_copy(
                built.at[:, pl.ds(start, here)],
                out_ref.at[:, pl.ds(start, here)],
                sems.at[start // here],
            )
        )
        copies[-1].start()
    for copy in copies:
        copy.wait()


def inverse(info, chunks, table, order, z_table, local_part, shape, per_tile, here):
    channels, cells_x, cells_y, length = shape
    return pl.pallas_call(
        functools.partial(inverse_kernel, len(chunks), per_tile, here),
        out_shape=jax.ShapeDtypeStruct(shape, jnp.bfloat16),
        in_specs=[IN_SMEM] + [IN_VMEM] * (4 + len(chunks)),
        out_specs=IN_HBM,
        scratch_shapes=[
            pltpu.VMEM((table.shape[2], order.shape[0]), jnp.float32),
            pltpu.VMEM((cells_x, cells_y, order.shape[1]), jnp.bfloat16),
            pltpu.VMEM(shape, jnp.bfloat16),
            pltpu.SemaphoreType.DMA((cells_x // here,)),
        ],
        compiler_params=params(28),
        cost_estimate=pl.CostEstimate(
            flops=2 * local_part.size * LANES, bytes_accessed=4 * local_part.size, transcendentals=0
        ),
        name="inverse",
    )(info, *resident(table, order, z_table, local_part), *chunks)


def flip(value, axes, size, r):
    return lax.ppermute(value, axes, [(i, i ^ r) for i in range(size)])


def body(field_in, grad_pre, spec_weight, point_weight):
    _, channels, cells_x, cells_y, cells_z = field_in.shape
    groups_x, groups_y = lax.axis_size("gx"), lax.axis_size("gy")
    groups, scenes = groups_x * groups_y, lax.axis_size("scene")
    group_axes = ("gx", "gy")
    total_x, total_y = cells_x * groups_x, cells_y * groups_y
    cells = cells_x * cells_y
    norm = float(total_x * total_y * cells_z) ** -0.5
    modes_xd, modes_yd = spec_weight.shape[:2]
    modes = modes_xd * modes_yd
    rows = -(-modes // 8) * 8
    half = LANES // (2 * channels)
    tiles = -(-MZ // half)
    block = channels // 4
    slot = 16
    per_tile = LANES // (2 * slot)
    sizes = (groups, groups_y, modes_xd, modes_yd, total_x, total_y)

    me = lax.axis_index(group_axes)
    at_x, at_y = lax.axis_index("gx"), lax.axis_index("gy")
    quad = at_x % 2 * 2 + at_y % 2
    base, turns = (jnp.asarray(t) for t in forward_table(rows, sizes, cells_x, cells_y))
    if groups * groups * rows * 2 * cells <= 1 << 24:
        inverse_t = jnp.asarray(
            np.stack([inverse_table(np, i, rows, sizes, cells_x, cells_y) for i in range(groups)])
        )
        inverse_at = me
    else:
        inverse_t = inverse_table(jnp, me, rows, sizes, cells_x, cells_y)[None]
        inverse_at = 0 * me
    forward_at = at_x // 2 * (groups_y // 2) + at_y // 2
    info = jnp.stack([me, quad, forward_at, inverse_at, lax.axis_index("scene")])

    regroup = jnp.asarray(regroup_table(channels, block, half))
    inverse_z = jnp.asarray(inverse_z_table(cells_z, per_tile, slot, norm))
    order = jnp.asarray(order_table(channels, tiles * half, per_tile, slot))
    lane = np.arange(LANES)
    spread = jnp.asarray(spread_table(channels, half, lane % channels))
    gather = jnp.asarray(gather_table(channels, LANES // channels))
    here = channels // scenes
    pair = np.arange(here * channels)
    kz_tile = LANES // (2 * block)
    pick = spread_table(here, kz_tile, pair // channels).reshape(LANES, kz_tile, -1)
    pick = jnp.asarray(pick.transpose(1, 0, 2))
    cell_rows, cell_columns = (jnp.asarray(t) for t in cell_tables(channels, per_tile, cells_y))
    scale = np.full((2, 4, kz_tile, 2 * block), 2.0 * norm, np.float32)
    scale[0, :, 0] = norm
    scale = jnp.asarray(scale.reshape(2, 4 * LANES))

    def cells_of(field):
        mine = along_z(info, field.reshape(channels, cells, cells_z), block)
        return [mine[0]] + [
            flip(mine[t], group_axes, groups, quad_offset(t, groups_y)) for t in range(1, 4)
        ]

    grad_cells = cells_of(grad_pre)
    field, _ = lax.optimization_barrier((field_in, grad_cells[0]))
    field_cells = cells_of(field)
    grad_sums, table = first_plane(info, grad_cells, base, turns, block)
    sums = second_plane(info, field_cells, table, grad_sums, groups, rows, block)
    got = {0: sums[0], 1: flip(sums[1], group_axes, groups, 1)}
    far = [r for r in range(groups - 1, 1, -1) if r % groups_y >= groups_y // 2]
    for r in far:
        got[r] = flip(sums[r], group_axes, groups, r)
    near = [r for r in range(2, groups) if r not in far]
    waiting, _ = lax.optimization_barrier(([sums[r] for r in near], got[1]))
    for r, value in zip(near, waiting):
        got[r] = flip(value, group_axes, groups, r)
    got = [got[r] for r in range(groups)]
    weight = spec_weight.reshape(modes, MZ, 2, channels * channels)
    weight = jnp.pad(weight.transpose(1, 2, 0, 3), ((0, 0), (0, 0), (0, rows - modes), (0, 0)))
    local_part = local(
        cell_rows,
        cell_columns,
        point_weight,
        grad_pre.reshape(channels, cells_x, cells_y, cells_z),
    )
    got, weight, local_part = lax.optimization_barrier((got, weight, local_part))
    over = 2 * MZ * block - LANES
    mode_grad, spectra = mix(
        info,
        got,
        scale,
        norm,
        regroup,
        spread,
        gather,
        weight,
        (tiles, rows, over, scenes, groups_y),
    )

    along_y = [mode_grad] + [None] * (groups_y - 1)
    for r in range(groups_y - 1, 0, -1):
        along_y[r] = flip(mode_grad, "gy", groups_y, r)
    gathered = list(along_y)
    for r in range(1, groups_x):
        for k, value in enumerate(along_y):
            if k == 1:
                gathered.append(flip(mode_grad, group_axes, groups, r * groups_y + k))
            else:
                gathered.append(flip(value, "gx", groups_x, r))

    got = [spectra[0]]
    for r in range(1, scenes):
        after = mode_grad if r == 2 else along_y[1] if r == 3 else along_y[-1]
        value, _ = lax.optimization_barrier((spectra[r], after))
        got.append(flip(value, "scene", scenes, r))
    spectra = got
    grad_field = inverse(
        info,
        gathered,
        inverse_t,
        order,
        inverse_z,
        local_part,
        (channels, cells_x, cells_y, cells_z),
        per_tile,
        2,
    )
    spectra, grad_field = lax.optimization_barrier((spectra, grad_field))
    grads = outer(spectra, spread, pick)
    grads = grads.reshape(rows, MZ, here * channels // LANES, 2, LANES)[:modes]
    grad_spec = grads.transpose(0, 1, 3, 2, 4).reshape(
        modes_xd, modes_yd, MZ, 2, here * channels
    )

    return grad_field[None], grad_spec


def solution(mesh):
    return jax.shard_map(
        body,
        mesh=mesh,
        in_specs=(
            P("scene", None, "gx", "gy", None),
            P("scene", None, "gx", "gy", None),
            P("gx", "gy", None, None, None),
            P(),
        ),
        out_specs=(P("scene", None, "gx", "gy", None), P("gx", "gy", None, None, "scene")),
        check_vma=False,
    )
```

```python
import functools
import math

import jax
import jax.numpy as jnp
import ml_dtypes
import numpy as np
from jax import lax
from jax.experimental import pallas as pl
from jax.experimental.pallas import tpu as pltpu
from jax.sharding import PartitionSpec as P

MX = 24
MY = 24
MZ = 13
LANES = 128
NT = (((1,), (1,)), ((), ()))
BF16 = ml_dtypes.bfloat16


def angles(xp, index, modes, positions, length):
    freq = xp.where(index < modes // 2, index, index - modes)
    turns = (freq[..., None] * positions) % length
    return turns.astype(np.float32) * np.float32(2.0 * math.pi / length)


def mode_angles(xp, rows, sizes, local_x, local_y):
    groups, groups_y, modes_xd, modes_yd, total_x, total_y = sizes
    owner = xp.repeat(xp.arange(groups, dtype=np.int32), rows)
    within = xp.tile(xp.arange(rows, dtype=np.int32), groups)
    kx = owner // groups_y * modes_xd + xp.minimum(within // modes_yd, modes_xd - 1)
    ky = owner % groups_y * modes_yd + within % modes_yd
    angle_x = angles(xp, kx, MX, local_x, total_x)
    angle_y = angles(xp, ky, MY, local_y, total_y)
    theta = (angle_x[:, :, None] + angle_y[:, None, :]).reshape(owner.shape[0], -1)
    return theta, (within < modes_xd * modes_yd)[:, None]


def device_cells(xp, me, groups_y, cells_x, cells_y):
    local_x = me // groups_y * cells_x + xp.arange(cells_x, dtype=np.int32)
    local_y = me % groups_y * cells_y + xp.arange(cells_y, dtype=np.int32)
    return local_x, local_y


def forward_table(rows, sizes, cells_x, cells_y):
    groups, groups_y = sizes[:2]
    theta, real = mode_angles(
        np, rows, sizes, *device_cells(np, np.int32(0), groups_y, cells_x, cells_y)
    )
    base = np.where(real, np.concatenate([np.cos(theta), np.sin(theta)], 1), np.float32(0))
    turns = []
    for x in range(0, groups // groups_y, 2):
        for y in range(0, groups_y, 2):
            turn = np.zeros((groups * rows, LANES), np.float32)
            for t in range(4):
                device = np.int32(x * groups_y + y + quad_offset(t, groups_y))
                local_x, local_y = device_cells(np, device, groups_y, cells_x, cells_y)
                angle, _ = mode_angles(np, rows, sizes, local_x[:1], local_y[:1])
                turn[:, 2 * t] = np.cos(angle[:, 0])
                turn[:, 2 * t + 1] = np.sin(angle[:, 0])
            turns.append(turn)
    return base, np.stack(turns)


def inverse_table(xp, me, rows, sizes, cells_x, cells_y):
    theta, real = mode_angles(
        xp, rows, sizes, *device_cells(xp, me, sizes[1], cells_x, cells_y)
    )
    cosine = xp.where(real, xp.cos(theta), np.float32(0))
    sine = xp.where(real, xp.sin(theta), np.float32(0))
    return xp.stack(split16(xp.concatenate([cosine.T, sine.T], 0)))


def quad_offset(t, groups_y):
    return t // 2 * groups_y + t % 2


def quad_of(r, groups_y):
    return r // groups_y % 2 * 2 + r % groups_y % 2


def split16(values):
    high = values.astype(BF16)
    low = (values - high.astype(np.float32)).astype(BF16)
    return high, low


def inverse_z_table(length, per_tile, slot, norm):
    modes, cells = np.arange(MZ, dtype=np.int32), np.arange(length, dtype=np.int32)
    theta = angles(np, modes, 2 * MZ, cells, length)
    parts = np.stack([np.cos(theta), -np.sin(theta)], 0) * np.float32(norm)
    table = np.zeros((per_tile, 2, slot, per_tile, length), np.float32)
    for c in range(per_tile):
        table[c, :, :MZ, c] = parts
    high, low = split16(table.reshape(LANES, per_tile * length))
    return np.concatenate([high, low], 0)


def order_table(channels, kz_pad, per_tile, slot):
    table = np.zeros((kz_pad, 2, channels, channels // per_tile, per_tile, 2, slot), np.float32)
    for kz in range(MZ):
        for part in range(2):
            for c in range(channels):
                table[kz, part, c, c // per_tile, c % per_tile, part, kz] = 1
    return table.reshape(kz_pad * 2 * channels, -1).astype(BF16)


def spread_table(channels, half, copies):
    table = np.zeros((half, 2, channels, half, 2, copies.shape[0]), np.float32)
    for h in range(half):
        for part in range(2):
            table[h, part, copies, h, part, np.arange(copies.shape[0])] = 1
    return table.reshape(half * 2 * channels, -1).astype(BF16)


def gather_table(channels, copies):
    table = np.zeros((channels, channels, copies, channels), np.float32)
    for i in range(channels):
        table[i, :, :, i] = 1
    return table.reshape(channels * channels, -1).astype(BF16)


def cell_tables(channels, per_tile, cells_y):
    rows = np.zeros((per_tile, channels // per_tile, cells_y, channels), np.float32)
    for c in range(channels):
        rows[c % per_tile, c // per_tile, :, c] = 1
    columns = np.repeat(np.eye(channels, dtype=np.float32), cells_y, 1)
    return rows.reshape(-1, channels).astype(BF16), columns.astype(BF16)


def regroup_table(channels, block, half):
    groups = channels // block
    kz_tile = LANES // (2 * block)
    table = np.zeros((groups, kz_tile, 2, block, kz_tile // half, half, 2, groups, block), np.float32)
    for g in range(groups):
        for kz in range(kz_tile):
            for part in range(2):
                for c in range(block):
                    table[g, kz, part, c, kz // half, kz % half, part, g, c] = 1
    return table.reshape(groups * LANES, -1).astype(BF16)


def params(mib):
    return pltpu.CompilerParams(vmem_limit_bytes=mib * 1024 * 1024)


IN_VMEM = pl.BlockSpec(memory_space=pltpu.VMEM)
IN_SMEM = pl.BlockSpec(memory_space=pltpu.SMEM)
IN_HBM = pl.BlockSpec(memory_space=pl.ANY)


def resident(*arrays):
    return [pltpu.with_memory_space_constraint(a, pltpu.VMEM) for a in arrays]


def along_z_kernel(info_ref, x_ref, *rest):
    outs, table = rest[:4], rest[4]
    block, span, length = table.shape
    padded = -(-2 * MZ // 16) * 16
    row = lax.broadcasted_iota(jnp.int32, (padded, length), 0)
    cell = lax.broadcasted_iota(jnp.int32, (padded, length), 1)
    theta = ((row // 2 * cell) % length).astype(jnp.float32) * (2.0 * math.pi / length)
    parts = jnp.where(row % 2 == 0, jnp.cos(theta), -jnp.sin(theta))
    row = lax.broadcasted_iota(jnp.int32, (span, padded), 0) // block
    repeat = (row == lax.broadcasted_iota(jnp.int32, (span, padded), 1)).astype(jnp.bfloat16)
    rows = jnp.dot(repeat, parts.astype(jnp.bfloat16), preferred_element_type=jnp.float32)
    channel = lax.broadcasted_iota(jnp.int32, rows.shape, 0) % block
    for c in range(block):
        table[c] = jnp.where(channel == c, rows, 0.0).astype(jnp.bfloat16)
    for t in range(4):
        first = jnp.bitwise_xor(info_ref[1], t) * block
        total = None
        for c in range(block):
            term = lax.dot_general(
                table[c], x_ref[first + c], NT, preferred_element_type=jnp.float32
            )
            total = term if total is None else total + term
        outs[t][...] = total.astype(jnp.bfloat16)


def along_z(info, field, block):
    channels, cells, length = field.shape
    span = 2 * MZ * block
    return pl.pallas_call(
        along_z_kernel,
        out_shape=[jax.ShapeDtypeStruct((span, cells), jnp.bfloat16)] * 4,
        in_specs=[IN_SMEM, IN_VMEM],
        out_specs=[IN_VMEM] * 4,
        scratch_shapes=[pltpu.VMEM((block, span, length), jnp.bfloat16)],
        compiler_params=params(12),
        cost_estimate=pl.CostEstimate(
            flops=2 * span * cells * length * channels,
            bytes_accessed=2 * field.size,
            transcendentals=0,
        ),
        name="along_z",
    )(info, *resident(field))


def place_cells(info_ref, sources, block, data):
    span, cells = sources[0].shape
    for t in range(4):
        place = jnp.bitwise_xor(info_ref[1], t)
        value = sources[t][...].astype(jnp.float32)
        turned = []
        for k in range(0, span, 2 * block):
            turned += [value[k + block : k + 2 * block], -value[k : k + block]]
        data[place, :, :cells] = sources[t][...]
        data[place, :, cells:] = jnp.concatenate(turned, 0).astype(jnp.bfloat16)


def sum_plane(table, data):
    total = None
    for device in range(4):
        for part in range(2):
            term = lax.dot_general(
                table[device, part], data[device], NT, preferred_element_type=jnp.float32
            )
            total = term if total is None else total + term
    return total


def first_plane_kernel(block, info_ref, base_ref, turn_ref, *refs):
    sources, (out_ref, table, data) = refs[:4], refs[4:]
    cells = sources[0].shape[1]
    place_cells(info_ref, sources, block, data)
    turns = turn_ref[info_ref[2]]
    cosine, sine = base_ref[:, :cells], base_ref[:, cells:]
    for device in range(4):
        turn_cos = turns[:, 2 * device : 2 * device + 1]
        turn_sin = turns[:, 2 * device + 1 : 2 * device + 2]
        both = (cosine * turn_cos - sine * turn_sin, sine * turn_cos + cosine * turn_sin)
        for k, values in enumerate(both):
            high = values.astype(jnp.bfloat16)
            table[device, 0, :, k * cells : (k + 1) * cells] = high
            low = (values - high.astype(jnp.float32)).astype(jnp.bfloat16)
            table[device, 1, :, k * cells : (k + 1) * cells] = low
    out_ref[...] = sum_plane(table, data)


def first_plane(info, sources, base, turns, block):
    span, cells = sources[0].shape
    modes = base.shape[0]
    return pl.pallas_call(
        functools.partial(first_plane_kernel, block),
        out_shape=[
            jax.ShapeDtypeStruct((modes, span), jnp.float32),
            jax.ShapeDtypeStruct((4, 2, modes, 2 * cells), jnp.bfloat16),
        ],
        in_specs=[IN_SMEM] + [IN_VMEM] * 6,
        out_specs=[IN_VMEM] * 2,
        scratch_shapes=[pltpu.VMEM((4, span, 2 * cells), jnp.bfloat16)],
        compiler_params=params(24),
        cost_estimate=pl.CostEstimate(
            flops=32 * cells * span * modes, bytes_accessed=4 * base.size, transcendentals=0
        ),
        name="first_plane",
    )(info, *resident(base, turns), *sources)


def tail_parts(rows):
    return next(k for k in (3, 2, 1) if rows % (8 * k) == 0)


def second_plane_kernel(groups, rows, block, info_ref, table_ref, other_ref, *refs):
    sources, outs, (sums, data) = refs[:4], refs[4 : 4 + groups], refs[4 + groups :]
    place_cells(info_ref, sources, block, data)
    sums[...] = sum_plane(table_ref, data)
    over = sums.shape[1] - LANES
    room = LANES - over
    parts = tail_parts(rows)
    step = rows // parts
    for r in range(groups):
        owner = jnp.bitwise_xor(info_ref[0], r)
        own = pl.ds(pl.multiple_of(owner * rows, 8), rows)
        first, second = other_ref[own], sums[own]
        mixed = jnp.concatenate([first[:, LANES:], second[:, LANES : LANES + room]], 1)
        tail = second[:, LANES + room :]
        tail = [tail[k * step : (k + 1) * step] for k in range(parts)]
        rest = LANES - parts * (over - room)
        tail = jnp.concatenate(tail + [jnp.zeros((step, rest), jnp.float32)], 1)
        whole = jnp.concatenate([first[:, :LANES], second[:, :LANES], mixed, tail], 0)
        outs[r][...] = whole.astype(jnp.bfloat16)


def second_plane(info, sources, table, other, groups, rows, block):
    span, cells = sources[0].shape
    modes = table.shape[2]
    chunk = jax.ShapeDtypeStruct((3 * rows + rows // tail_parts(rows), LANES), jnp.bfloat16)
    return pl.pallas_call(
        functools.partial(second_plane_kernel, groups, rows, block),
        out_shape=[chunk] * groups,
        in_specs=[IN_SMEM] + [IN_VMEM] * 6,
        out_specs=[IN_VMEM] * groups,
        scratch_shapes=[
            pltpu.VMEM((modes, span), jnp.float32),
            pltpu.VMEM((4, span, 2 * cells), jnp.bfloat16),
        ],
        compiler_params=params(24),
        cost_estimate=pl.CostEstimate(
            flops=32 * cells * span * modes, bytes_accessed=2 * table.size, transcendentals=0
        ),
        name="second_plane",
    )(info, *resident(table), other, *sources)


def mix_kernel(groups, groups_y, over, scale, info_ref, *refs):
    (scale_ref, regroup_ref), consts, refs = refs[:2], refs[2:5], refs[5:]
    chunks, mode_ref, outs, (held, low_ref) = refs[:groups], refs[groups], refs[groups + 1 : -2], refs[-2:]
    rows = held.shape[2]
    parts = tail_parts(rows)
    room = LANES - over
    left = over - room
    for t in range(4):
        place = jnp.bitwise_xor(info_ref[1], t)
        mine = [c for r, c in enumerate(chunks) if quad_of(r, groups_y) == t]
        total = mine[0][...].astype(jnp.float32)
        for ref in mine[1:]:
            total = total + ref[...].astype(jnp.float32)
        mixed, tail = total[2 * rows : 3 * rows], total[3 * rows :]
        tail = jnp.concatenate([tail[:, k * left : (k + 1) * left] for k in range(parts)], 0)
        zeros = jnp.zeros((rows, room), jnp.float32)
        held[place, 0] = total[:rows]
        held[place, 1] = jnp.concatenate([mixed[:, :over], zeros], 1)
        held[place, 2] = total[rows : 2 * rows]
        held[place, 3] = jnp.concatenate([mixed[:, over:], tail, zeros], 1)
    tiles = outs[0].shape[0] - 2
    for j in range(2):
        values = jnp.concatenate([held[g, j] for g in range(4)], 1) * scale_ref[j : j + 1]
        high, low = (
            jnp.dot(v, regroup_ref[...], preferred_element_type=jnp.float32).astype(jnp.bfloat16)
            for v in split_rows(values)
        )
        for k in range(4):
            if j * 4 + k < tiles:
                low_ref[j * 4 + k] = low[:, k * LANES : (k + 1) * LANES]
                for out in outs:
                    out[j * 4 + k] = high[:, k * LANES : (k + 1) * LANES]
    for r, out in enumerate(outs):
        for j in range(2):
            value = held[jnp.bitwise_xor(info_ref[4], r), 2 + j] * scale
            out[tiles + j] = value.astype(jnp.bfloat16)
    mode_gradients(*consts, outs[0], low_ref, mode_ref)


def packed_rows(tiles, rows, used):
    top = -(-rows // 16) * 8 if 2 * used <= LANES else rows
    return top, (tiles - 1) * rows + top


def split_rows(values):
    high = values.astype(jnp.bfloat16)
    return high, (values - high.astype(jnp.float32)).astype(jnp.bfloat16)


def mode_gradients(spread_ref, gather_ref, w_ref, s_ref, low_ref, out_ref):
    tiles, rows = s_ref.shape[0] - 2, s_ref.shape[1]
    last, _, _, width = w_ref.shape
    half = spread_ref.shape[1] // (2 * LANES)
    for tile in range(tiles):
        wide = jnp.dot(s_ref[tile], spread_ref[...], preferred_element_type=jnp.float32)
        wide += jnp.dot(low_ref[tile], spread_ref[...], preferred_element_type=jnp.float32)
        products = []
        for h in range(half):
            kz = tile * half + h
            if kz >= last:
                continue
            out_re = wide[:, (2 * h) * LANES : (2 * h + 1) * LANES]
            out_im = wide[:, (2 * h + 1) * LANES : (2 * h + 2) * LANES]
            real, imag = [], []
            for k in range(width // LANES):
                lane = slice(k * LANES, (k + 1) * LANES)
                w_re = w_ref[kz, 0, :, lane].astype(jnp.float32)
                w_im = w_ref[kz, 1, :, lane].astype(jnp.float32)
                real.append(w_re * out_re + w_im * out_im)
                imag.append(w_re * out_im - w_im * out_re)
            products += [jnp.concatenate(real, 1), jnp.concatenate(imag, 1)]
        high, low = split_rows(jnp.concatenate(products, 0))
        sums = jnp.dot(high, gather_ref[...], preferred_element_type=jnp.float32)
        sums += jnp.dot(low, gather_ref[...], preferred_element_type=jnp.float32)
        which = lax.broadcasted_iota(jnp.int32, (rows, LANES), 1) // (LANES // (2 * half))
        out = sums[:rows]
        for k in range(1, len(products)):
            out = jnp.where(which == k, sums[k * rows : (k + 1) * rows], out)
        out = jnp.where(which < len(products), out, 0.0)
        top = out_ref.shape[0] - (tiles - 1) * rows
        if tile == tiles - 1 and top < rows:
            lower = out[top:]
            if 2 * top > rows:
                zeros = jnp.zeros((2 * top - rows, LANES), jnp.float32)
                lower = jnp.concatenate([lower, zeros], 0)
            out = jnp.concatenate([out[:top, : LANES // 2], lower[:, : LANES // 2]], 1)
        out_ref[tile * rows : tile * rows + out.shape[0]] = out.astype(jnp.bfloat16)


def mix(info, chunks, scale, norm, regroup, spread, gather, weight, sizes):
    tiles, rows, over, scenes, groups_y = sizes
    half = spread.shape[1] // (2 * LANES)
    used = (MZ - (tiles - 1) * half) * spread.shape[0] // half
    out = jax.ShapeDtypeStruct((tiles + 2, rows, LANES), jnp.bfloat16)
    modes = jax.ShapeDtypeStruct((packed_rows(tiles, rows, used)[1], LANES), jnp.bfloat16)
    results = pl.pallas_call(
        functools.partial(mix_kernel, len(chunks), groups_y, over, norm),
        out_shape=[modes] + [out] * scenes,
        in_specs=[IN_SMEM] + [IN_VMEM] * (5 + len(chunks)),
        out_specs=[IN_VMEM] * (1 + scenes),
        scratch_shapes=[
            pltpu.VMEM((4, 4, rows, LANES), jnp.float32),
            pltpu.VMEM((tiles, rows, LANES), jnp.bfloat16),
        ],
        compiler_params=params(24),
        cost_estimate=pl.CostEstimate(
            flops=8 * tiles * rows * gather.size, bytes_accessed=2 * weight.size, transcendentals=0
        ),
        name="mix",
    )(info, *resident(scale, regroup, spread, gather, weight), *chunks)
    return results[0], results[1:]


def outer_kernel(scenes, spread_ref, pick_ref, *refs):
    spectra, out_ref = refs[:scenes], refs[scenes]
    rows = spectra[0].shape[1]
    copies = pick_ref.shape[2] // (2 * LANES)
    last = out_ref.shape[0] // (2 * copies * rows)
    wide = copies * LANES
    half = spread_ref.shape[1] // (2 * LANES)
    per_tile = pick_ref.shape[0]
    tiles = spectra[0].shape[0] - 2
    for kz in range(last):
        if kz % half == 0:
            grads = jnp.dot(
                jnp.concatenate([ref[kz // half] for ref in spectra], 0),
                spread_ref[...],
                preferred_element_type=jnp.float32,
            )
        if kz % per_tile == 0:
            field = jnp.concatenate([ref[tiles + kz // per_tile] for ref in spectra], 0)
        hats = jnp.dot(field, pick_ref[kz % per_tile], preferred_element_type=jnp.float32)
        lane = 2 * (kz % half) * LANES
        for k in range(wide // LANES):
            real, imag = 0.0, 0.0
            for s in range(scenes):
                here = slice(s * rows, (s + 1) * rows)
                hat_re = hats[here, k * LANES : (k + 1) * LANES]
                hat_im = hats[here, wide + k * LANES : wide + (k + 1) * LANES]
                out_re = grads[here, lane : lane + LANES]
                out_im = grads[here, lane + LANES : lane + 2 * LANES]
                real += out_re * hat_re + out_im * hat_im
                imag += out_im * hat_re - out_re * hat_im
            for part, value in enumerate((real, imag)):
                first = (kz * copies + k) * 2 + part
                out_ref[pl.ds(first, rows, stride=2 * copies * last), :] = value


def outer(spectra, spread, pick):
    tiles, rows, _ = spectra[0].shape
    wide = pick.shape[2] // 2
    return pl.pallas_call(
        functools.partial(outer_kernel, len(spectra)),
        out_shape=jax.ShapeDtypeStruct((rows * MZ * wide // LANES * 2, LANES), jnp.float32),
        in_specs=[IN_VMEM] * (2 + len(spectra)),
        out_specs=IN_VMEM,
        compiler_params=params(16),
        cost_estimate=pl.CostEstimate(
            flops=2 * tiles * rows * 4 * LANES * 12 * LANES,
            bytes_accessed=16 * tiles * rows * wide + 8 * tiles * rows * LANES * len(spectra),
            transcendentals=0,
        ),
        name="outer",
    )(*resident(spread, pick), *spectra)


def local_kernel(row_ref, column_ref, point_ref, grad_ref, out_ref, mixing):
    channels, cells_x, cells_y, length = grad_ref.shape
    picked = lax.dot_general(row_ref[...], point_ref[...], NT, preferred_element_type=jnp.float32)
    spread = jnp.dot(
        picked.astype(jnp.bfloat16), column_ref[...], preferred_element_type=jnp.float32
    )
    row = lax.broadcasted_iota(jnp.int32, spread.shape, 0) % cells_y
    column = lax.broadcasted_iota(jnp.int32, spread.shape, 1) % cells_y
    mixing[...] = jnp.where(row == column, spread, 0.0).astype(jnp.bfloat16)

    @pl.loop(0, cells_x, step=4)
    def _(start):
        for x in range(4):
            out_ref[start + x] = jnp.dot(
                mixing[...],
                grad_ref[:, start + x].reshape(channels * cells_y, length),
                preferred_element_type=jnp.float32,
            ).astype(out_ref.dtype)


def local(cell_rows, cell_columns, point, grad):
    channels, cells_x, cells_y, length = grad.shape
    width = channels * cells_y
    return pl.pallas_call(
        local_kernel,
        out_shape=jax.ShapeDtypeStruct((cells_x, width, length), jnp.bfloat16),
        in_specs=[IN_VMEM] * 4,
        out_specs=IN_VMEM,
        scratch_shapes=[pltpu.VMEM((width, width), jnp.bfloat16)],
        compiler_params=params(16),
        cost_estimate=pl.CostEstimate(
            flops=2 * grad.size * width, bytes_accessed=4 * grad.size, transcendentals=0
        ),
        name="local",
    )(*resident(cell_rows, cell_columns, point, grad))


def inverse_kernel(groups, per_tile, here, info_ref, t_ref, order_ref, z_ref, local_ref, *refs):
    chunks, (out_ref, modes, held, built, sems) = refs[:groups], refs[groups:]
    channels, cells_x, cells_y, length = built.shape
    rows = modes.shape[0] // groups
    tiles = channels // per_tile
    last = modes.shape[1] // LANES - 1
    top = chunks[0].shape[0] - last * rows
    for r in range(groups):
        own = pl.ds(pl.multiple_of(jnp.bitwise_xor(info_ref[0], r) * rows, 8), rows)
        for j in range(last):
            value = chunks[r][j * rows : (j + 1) * rows]
            modes[own, j * LANES : (j + 1) * LANES] = value.astype(jnp.float32)
        value = chunks[r][last * rows :].astype(jnp.float32)
        if top < rows:
            middle = LANES // 2
            value = jnp.concatenate([value[:, :middle], value[: rows - top, middle:]], 0)
            value = jnp.concatenate([value, jnp.zeros_like(value)], 1)
        modes[own, last * LANES :] = value
    gathered = modes[...].astype(jnp.bfloat16)
    sums = jnp.dot(t_ref[info_ref[3], 0], gathered, preferred_element_type=jnp.float32)
    sums += jnp.dot(t_ref[info_ref[3], 1], gathered, preferred_element_type=jnp.float32)
    cells = sums.shape[0] // 2
    cosine, sine = sums[:cells], sums[cells:]
    wide = sine.shape[1]
    lane = lax.broadcasted_iota(jnp.int32, sine.shape, 1)
    first = lane % (2 * channels) < channels
    turned = jnp.where(
        first, -pltpu.roll(sine, wide - channels, 1), pltpu.roll(sine, channels, 1)
    )
    back = (cosine + turned).astype(jnp.bfloat16)
    ordered = jnp.dot(back, order_ref[...], preferred_element_type=jnp.float32)
    held[...] = ordered.astype(jnp.bfloat16).reshape(held.shape)

    span = tiles * cells_y
    copies = []
    for start in range(0, cells_x, here):
        stack = []
        for x in range(start, start + here):
            back = held[x]
            stack += [back[:, k * LANES : (k + 1) * LANES] for k in range(tiles)]
        stack = jnp.concatenate(stack, 0)
        spectral = jnp.dot(
            jnp.concatenate([stack, stack], 1), z_ref[...], preferred_element_type=jnp.float32
        )
        for x in range(here):
            for j in range(per_tile):
                both = (
                    spectral[x * span : (x + 1) * span, j * length : (j + 1) * length]
                    + local_ref[start + x, j * span : (j + 1) * span].astype(jnp.float32)
                ).astype(jnp.bfloat16)
                for k in range(tiles):
                    built[k * per_tile + j, start + x] = both[k * cells_y : (k + 1) * cells_y]
        copies.append(
            pltpu.make_async_copy(
                built.at[:, pl.ds(start, here)],
                out_ref.at[:, pl.ds(start, here)],
                sems.at[start // here],
            )
        )
        copies[-1].start()
    for copy in copies:
        copy.wait()


def inverse(info, chunks, table, order, z_table, local_part, shape, per_tile, here):
    channels, cells_x, cells_y, length = shape
    return pl.pallas_call(
        functools.partial(inverse_kernel, len(chunks), per_tile, here),
        out_shape=jax.ShapeDtypeStruct(shape, jnp.bfloat16),
        in_specs=[IN_SMEM] + [IN_VMEM] * (4 + len(chunks)),
        out_specs=IN_HBM,
        scratch_shapes=[
            pltpu.VMEM((table.shape[3], order.shape[0]), jnp.float32),
            pltpu.VMEM((cells_x, cells_y, order.shape[1]), jnp.bfloat16),
            pltpu.VMEM(shape, jnp.bfloat16),
            pltpu.SemaphoreType.DMA((cells_x // here,)),
        ],
        compiler_params=params(28),
        cost_estimate=pl.CostEstimate(
            flops=2 * local_part.size * LANES, bytes_accessed=4 * local_part.size, transcendentals=0
        ),
        name="inverse",
    )(info, *resident(table, order, z_table, local_part), *chunks)


def flip(value, axes, size, r):
    return lax.ppermute(value, axes, [(i, i ^ r) for i in range(size)])


def body(field_in, grad_pre, spec_weight, point_weight):
    _, channels, cells_x, cells_y, cells_z = field_in.shape
    groups_x, groups_y = lax.axis_size("gx"), lax.axis_size("gy")
    groups, scenes = groups_x * groups_y, lax.axis_size("scene")
    group_axes = ("gx", "gy")
    total_x, total_y = cells_x * groups_x, cells_y * groups_y
    cells = cells_x * cells_y
    norm = float(total_x * total_y * cells_z) ** -0.5
    modes_xd, modes_yd = spec_weight.shape[:2]
    modes = modes_xd * modes_yd
    rows = -(-modes // 8) * 8
    half = LANES // (2 * channels)
    tiles = -(-MZ // half)
    block = channels // 4
    slot = 16
    per_tile = LANES // (2 * slot)
    sizes = (groups, groups_y, modes_xd, modes_yd, total_x, total_y)

    me = lax.axis_index(group_axes)
    at_x, at_y = lax.axis_index("gx"), lax.axis_index("gy")
    quad = at_x % 2 * 2 + at_y % 2
    base, turns = (jnp.asarray(t) for t in forward_table(rows, sizes, cells_x, cells_y))
    if groups * groups * rows * 2 * cells <= 1 << 24:
        inverse_t = jnp.asarray(
            np.stack([inverse_table(np, i, rows, sizes, cells_x, cells_y) for i in range(groups)])
        )
        inverse_at = me
    else:
        inverse_t = inverse_table(jnp, me, rows, sizes, cells_x, cells_y)[None]
        inverse_at = 0 * me
    forward_at = at_x // 2 * (groups_y // 2) + at_y // 2
    info = jnp.stack([me, quad, forward_at, inverse_at, lax.axis_index("scene")])

    regroup = jnp.asarray(regroup_table(channels, block, half))
    inverse_z = jnp.asarray(inverse_z_table(cells_z, per_tile, slot, norm))
    order = jnp.asarray(order_table(channels, tiles * half, per_tile, slot))
    lane = np.arange(LANES)
    spread = jnp.asarray(spread_table(channels, half, lane % channels))
    gather = jnp.asarray(gather_table(channels, LANES // channels))
    here = channels // scenes
    pair = np.arange(here * channels)
    kz_tile = LANES // (2 * block)
    pick = spread_table(here, kz_tile, pair // channels).reshape(LANES, kz_tile, -1)
    pick = jnp.asarray(pick.transpose(1, 0, 2))
    cell_rows, cell_columns = (jnp.asarray(t) for t in cell_tables(channels, per_tile, cells_y))
    scale = np.full((2, 4, kz_tile, 2 * block), 2.0 * norm, np.float32)
    scale[0, :, 0] = norm
    scale = jnp.asarray(scale.reshape(2, 4 * LANES))

    def cells_of(field):
        mine = along_z(info, field.reshape(channels, cells, cells_z), block)
        return [mine[0]] + [
            flip(mine[t], group_axes, groups, quad_offset(t, groups_y)) for t in range(1, 4)
        ]

    grad_cells = cells_of(grad_pre)
    field, _ = lax.optimization_barrier((field_in, grad_cells[0]))
    field_cells = cells_of(field)
    grad_sums, table = first_plane(info, grad_cells, base, turns, block)
    sums = second_plane(info, field_cells, table, grad_sums, groups, rows, block)
    got = {0: sums[0], 1: flip(sums[1], group_axes, groups, 1)}
    far = [r for r in range(groups - 1, 1, -1) if r % groups_y >= groups_y // 2]
    for r in far:
        got[r] = flip(sums[r], group_axes, groups, r)
    near = [r for r in range(2, groups) if r not in far]
    waiting, _ = lax.optimization_barrier(([sums[r] for r in near], got[1]))
    for r, value in zip(near, waiting):
        got[r] = flip(value, group_axes, groups, r)
    got = [got[r] for r in range(groups)]
    weight = spec_weight.reshape(modes, MZ, 2, channels * channels)
    weight = jnp.pad(weight.transpose(1, 2, 0, 3), ((0, 0), (0, 0), (0, rows - modes), (0, 0)))
    local_part = local(
        cell_rows,
        cell_columns,
        point_weight,
        grad_pre.reshape(channels, cells_x, cells_y, cells_z),
    )
    got, weight, local_part = lax.optimization_barrier((got, weight, local_part))
    over = 2 * MZ * block - LANES
    mode_grad, spectra = mix(
        info,
        got,
        scale,
        norm,
        regroup,
        spread,
        gather,
        weight,
        (tiles, rows, over, scenes, groups_y),
    )

    along_y = [mode_grad] + [None] * (groups_y - 1)
    for r in range(groups_y - 1, 0, -1):
        along_y[r] = flip(mode_grad, "gy", groups_y, r)
    gathered = list(along_y)
    for r in range(1, groups_x):
        for k, value in enumerate(along_y):
            if k == 1:
                gathered.append(flip(mode_grad, group_axes, groups, r * groups_y + k))
            else:
                gathered.append(flip(value, "gx", groups_x, r))

    got = [spectra[0]]
    for r in range(1, scenes):
        after = mode_grad if r == 2 else along_y[1] if r == 3 else along_y[-1]
        value, _ = lax.optimization_barrier((spectra[r], after))
        got.append(flip(value, "scene", scenes, r))
    spectra = got
    grad_field = inverse(
        info,
        gathered,
        inverse_t,
        order,
        inverse_z,
        local_part,
        (channels, cells_x, cells_y, cells_z),
        per_tile,
        2,
    )
    spectra, grad_field = lax.optimization_barrier((spectra, grad_field))
    grads = outer(spectra, spread, pick)
    grads = grads.reshape(rows, MZ, here * channels // LANES, 2, LANES)[:modes]
    grad_spec = grads.transpose(0, 1, 3, 2, 4).reshape(
        modes_xd, modes_yd, MZ, 2, here * channels
    )

    return grad_field[None], grad_spec


def solution(mesh):
    return jax.shard_map(
        body,
        mesh=mesh,
        in_specs=(
            P("scene", None, "gx", "gy", None),
            P("scene", None, "gx", "gy", None),
            P("gx", "gy", None, None, None),
            P(),
        ),
        out_specs=(P("scene", None, "gx", "gy", None), P("gx", "gy", None, None, "scene")),
        check_vma=False,
    )
```

```python
import functools
import math

import jax
import jax.numpy as jnp
import ml_dtypes
import numpy as np
from jax import lax
from jax.experimental import pallas as pl
from jax.experimental.pallas import tpu as pltpu
from jax.sharding import PartitionSpec as P

MX = 24
MY = 24
MZ = 13
LANES = 128
NT = (((1,), (1,)), ((), ()))
BF16 = ml_dtypes.bfloat16


def angles(xp, index, modes, positions, length):
    freq = xp.where(index < modes // 2, index, index - modes)
    turns = (freq[..., None] * positions) % length
    return turns.astype(np.float32) * np.float32(2.0 * math.pi / length)


def mode_angles(xp, rows, sizes, local_x, local_y):
    groups, groups_y, modes_xd, modes_yd, total_x, total_y = sizes
    owner = xp.repeat(xp.arange(groups, dtype=np.int32), rows)
    within = xp.tile(xp.arange(rows, dtype=np.int32), groups)
    kx = owner // groups_y * modes_xd + xp.minimum(within // modes_yd, modes_xd - 1)
    ky = owner % groups_y * modes_yd + within % modes_yd
    angle_x = angles(xp, kx, MX, local_x, total_x)
    angle_y = angles(xp, ky, MY, local_y, total_y)
    theta = (angle_x[:, :, None] + angle_y[:, None, :]).reshape(owner.shape[0], -1)
    return theta, (within < modes_xd * modes_yd)[:, None]


def device_cells(xp, me, groups_y, cells_x, cells_y):
    local_x = me // groups_y * cells_x + xp.arange(cells_x, dtype=np.int32)
    local_y = me % groups_y * cells_y + xp.arange(cells_y, dtype=np.int32)
    return local_x, local_y


def forward_table(rows, sizes, cells_x, cells_y):
    groups, groups_y = sizes[:2]
    theta, real = mode_angles(
        np, rows, sizes, *device_cells(np, np.int32(0), groups_y, cells_x, cells_y)
    )
    base = np.where(real, np.concatenate([np.cos(theta), np.sin(theta)], 1), np.float32(0))
    turns = []
    for x in range(0, groups // groups_y, 2):
        for y in range(0, groups_y, 2):
            turn = np.zeros((groups * rows, LANES), np.float32)
            for t in range(4):
                device = np.int32(x * groups_y + y + quad_offset(t, groups_y))
                local_x, local_y = device_cells(np, device, groups_y, cells_x, cells_y)
                angle, _ = mode_angles(np, rows, sizes, local_x[:1], local_y[:1])
                turn[:, 2 * t] = np.cos(angle[:, 0])
                turn[:, 2 * t + 1] = np.sin(angle[:, 0])
            turns.append(turn)
    return base, np.stack(turns)


def inverse_table(xp, me, rows, sizes, cells_x, cells_y):
    theta, real = mode_angles(
        xp, rows, sizes, *device_cells(xp, me, sizes[1], cells_x, cells_y)
    )
    cosine = xp.where(real, xp.cos(theta), np.float32(0))
    sine = xp.where(real, xp.sin(theta), np.float32(0))
    return xp.concatenate(split16(xp.concatenate([cosine.T, sine.T], 0)), 1)


def quad_offset(t, groups_y):
    return t // 2 * groups_y + t % 2


def quad_of(r, groups_y):
    return r // groups_y % 2 * 2 + r % groups_y % 2


def split16(values):
    high = values.astype(BF16)
    low = (values - high.astype(np.float32)).astype(BF16)
    return high, low


def inverse_z_table(length, per_tile, slot, norm):
    modes, cells = np.arange(MZ, dtype=np.int32), np.arange(length, dtype=np.int32)
    theta = angles(np, modes, 2 * MZ, cells, length)
    parts = np.stack([np.cos(theta), -np.sin(theta)], 0) * np.float32(norm)
    table = np.zeros((per_tile, 2, slot, per_tile, length), np.float32)
    for c in range(per_tile):
        table[c, :, :MZ, c] = parts
    high, low = split16(table.reshape(LANES, per_tile * length))
    return np.concatenate([high, low], 0)


def order_table(channels, kz_pad, per_tile, slot):
    table = np.zeros((kz_pad, 2, channels, channels // per_tile, per_tile, 2, slot), np.float32)
    for kz in range(MZ):
        for part in range(2):
            for c in range(channels):
                table[kz, part, c, c // per_tile, c % per_tile, part, kz] = 1
    return table.reshape(kz_pad * 2 * channels, -1).astype(BF16)


def spread_table(channels, half, copies):
    table = np.zeros((half, 2, channels, half, 2, copies.shape[0]), np.float32)
    for h in range(half):
        for part in range(2):
            table[h, part, copies, h, part, np.arange(copies.shape[0])] = 1
    return table.reshape(half * 2 * channels, -1).astype(BF16)


def gather_table(channels, copies):
    table = np.zeros((channels, channels, copies, channels), np.float32)
    for i in range(channels):
        table[i, :, :, i] = 1
    return table.reshape(channels * channels, -1).astype(BF16)


def cell_tables(channels, per_tile, cells_y):
    rows = np.zeros((per_tile, channels // per_tile, cells_y, channels), np.float32)
    for c in range(channels):
        rows[c % per_tile, c // per_tile, :, c] = 1
    columns = np.repeat(np.eye(channels, dtype=np.float32), cells_y, 1)
    return rows.reshape(-1, channels).astype(BF16), columns.astype(BF16)


def regroup_table(channels, block, half):
    groups = channels // block
    kz_tile = LANES // (2 * block)
    table = np.zeros((groups, kz_tile, 2, block, kz_tile // half, half, 2, groups, block), np.float32)
    for g in range(groups):
        for kz in range(kz_tile):
            for part in range(2):
                for c in range(block):
                    table[g, kz, part, c, kz // half, kz % half, part, g, c] = 1
    return table.reshape(groups * LANES, -1).astype(BF16)


def params(mib):
    return pltpu.CompilerParams(vmem_limit_bytes=mib * 1024 * 1024)


IN_VMEM = pl.BlockSpec(memory_space=pltpu.VMEM)
IN_SMEM = pl.BlockSpec(memory_space=pltpu.SMEM)
IN_HBM = pl.BlockSpec(memory_space=pl.ANY)


def resident(*arrays):
    return [pltpu.with_memory_space_constraint(a, pltpu.VMEM) for a in arrays]


def along_z_kernel(info_ref, x_ref, *rest):
    outs, table = rest[:4], rest[4]
    block, span, length = table.shape
    padded = -(-2 * MZ // 16) * 16
    row = lax.broadcasted_iota(jnp.int32, (padded, length), 0)
    cell = lax.broadcasted_iota(jnp.int32, (padded, length), 1)
    theta = ((row // 2 * cell) % length).astype(jnp.float32) * (2.0 * math.pi / length)
    parts = jnp.where(row % 2 == 0, jnp.cos(theta), -jnp.sin(theta))
    row = lax.broadcasted_iota(jnp.int32, (span, padded), 0) // block
    repeat = (row == lax.broadcasted_iota(jnp.int32, (span, padded), 1)).astype(jnp.bfloat16)
    rows = jnp.dot(repeat, parts.astype(jnp.bfloat16), preferred_element_type=jnp.float32)
    channel = lax.broadcasted_iota(jnp.int32, rows.shape, 0) % block
    for c in range(block):
        table[c] = jnp.where(channel == c, rows, 0.0).astype(jnp.bfloat16)
    for t in range(4):
        first = jnp.bitwise_xor(info_ref[1], t) * block
        total = None
        for c in range(block):
            term = lax.dot_general(
                table[c], x_ref[first + c], NT, preferred_element_type=jnp.float32
            )
            total = term if total is None else total + term
        outs[t][...] = total.astype(jnp.bfloat16)


def along_z(info, field, block):
    channels, cells, length = field.shape
    span = 2 * MZ * block
    return pl.pallas_call(
        along_z_kernel,
        out_shape=[jax.ShapeDtypeStruct((span, cells), jnp.bfloat16)] * 4,
        in_specs=[IN_SMEM, IN_VMEM],
        out_specs=[IN_VMEM] * 4,
        scratch_shapes=[pltpu.VMEM((block, span, length), jnp.bfloat16)],
        compiler_params=params(12),
        cost_estimate=pl.CostEstimate(
            flops=2 * span * cells * length * channels,
            bytes_accessed=2 * field.size,
            transcendentals=0,
        ),
        name="along_z",
    )(info, *resident(field))


def place_cells(info_ref, sources, block, data):
    span, cells = sources[0].shape
    for t in range(4):
        place = jnp.bitwise_xor(info_ref[1], t)
        value = sources[t][...].astype(jnp.float32)
        turned = []
        for k in range(0, span, 2 * block):
            turned += [value[k + block : k + 2 * block], -value[k : k + block]]
        data[place, :, :cells] = sources[t][...]
        data[place, :, cells:] = jnp.concatenate(turned, 0).astype(jnp.bfloat16)


def sum_plane(table, data):
    total = None
    for device in range(4):
        for part in range(2):
            term = lax.dot_general(
                table[device, part], data[device], NT, preferred_element_type=jnp.float32
            )
            total = term if total is None else total + term
    return total


def first_plane_kernel(block, info_ref, base_ref, turn_ref, *refs):
    sources, (out_ref, table, data) = refs[:4], refs[4:]
    cells = sources[0].shape[1]
    place_cells(info_ref, sources, block, data)
    turns = turn_ref[info_ref[2]]
    cosine, sine = base_ref[:, :cells], base_ref[:, cells:]
    for device in range(4):
        turn_cos = turns[:, 2 * device : 2 * device + 1]
        turn_sin = turns[:, 2 * device + 1 : 2 * device + 2]
        both = (cosine * turn_cos - sine * turn_sin, sine * turn_cos + cosine * turn_sin)
        for k, values in enumerate(both):
            high = values.astype(jnp.bfloat16)
            table[device, 0, :, k * cells : (k + 1) * cells] = high
            low = (values - high.astype(jnp.float32)).astype(jnp.bfloat16)
            table[device, 1, :, k * cells : (k + 1) * cells] = low
    out_ref[...] = sum_plane(table, data)


def first_plane(info, sources, base, turns, block):
    span, cells = sources[0].shape
    modes = base.shape[0]
    return pl.pallas_call(
        functools.partial(first_plane_kernel, block),
        out_shape=[
            jax.ShapeDtypeStruct((modes, span), jnp.float32),
            jax.ShapeDtypeStruct((4, 2, modes, 2 * cells), jnp.bfloat16),
        ],
        in_specs=[IN_SMEM] + [IN_VMEM] * 6,
        out_specs=[IN_VMEM] * 2,
        scratch_shapes=[pltpu.VMEM((4, span, 2 * cells), jnp.bfloat16)],
        compiler_params=params(24),
        cost_estimate=pl.CostEstimate(
            flops=32 * cells * span * modes, bytes_accessed=4 * base.size, transcendentals=0
        ),
        name="first_plane",
    )(info, *resident(base, turns), *sources)


def tail_parts(rows):
    return next(k for k in (3, 2, 1) if rows % (8 * k) == 0)


def second_plane_kernel(groups, rows, block, info_ref, table_ref, other_ref, *refs):
    sources, outs, (sums, data) = refs[:4], refs[4 : 4 + groups], refs[4 + groups :]
    place_cells(info_ref, sources, block, data)
    sums[...] = sum_plane(table_ref, data)
    over = sums.shape[1] - LANES
    room = LANES - over
    parts = tail_parts(rows)
    step = rows // parts
    for r in range(groups):
        owner = jnp.bitwise_xor(info_ref[0], r)
        own = pl.ds(pl.multiple_of(owner * rows, 8), rows)
        first, second = other_ref[own], sums[own]
        mixed = jnp.concatenate([first[:, LANES:], second[:, LANES : LANES + room]], 1)
        tail = second[:, LANES + room :]
        tail = [tail[k * step : (k + 1) * step] for k in range(parts)]
        rest = LANES - parts * (over - room)
        tail = jnp.concatenate(tail + [jnp.zeros((step, rest), jnp.float32)], 1)
        whole = jnp.concatenate([first[:, :LANES], second[:, :LANES], mixed, tail], 0)
        outs[r][...] = whole.astype(jnp.bfloat16)


def second_plane(info, sources, table, other, groups, rows, block):
    span, cells = sources[0].shape
    modes = table.shape[2]
    chunk = jax.ShapeDtypeStruct((3 * rows + rows // tail_parts(rows), LANES), jnp.bfloat16)
    return pl.pallas_call(
        functools.partial(second_plane_kernel, groups, rows, block),
        out_shape=[chunk] * groups,
        in_specs=[IN_SMEM] + [IN_VMEM] * 6,
        out_specs=[IN_VMEM] * groups,
        scratch_shapes=[
            pltpu.VMEM((modes, span), jnp.float32),
            pltpu.VMEM((4, span, 2 * cells), jnp.bfloat16),
        ],
        compiler_params=params(24),
        cost_estimate=pl.CostEstimate(
            flops=32 * cells * span * modes, bytes_accessed=2 * table.size, transcendentals=0
        ),
        name="second_plane",
    )(info, *resident(table), other, *sources)


def mix_kernel(groups, groups_y, over, scale, info_ref, *refs):
    (scale_ref, regroup_ref), consts, refs = refs[:2], refs[2:5], refs[5:]
    chunks, mode_ref, outs, (held, low_ref) = refs[:groups], refs[groups], refs[groups + 1 : -2], refs[-2:]
    rows = held.shape[2]
    parts = tail_parts(rows)
    room = LANES - over
    left = over - room
    for t in range(4):
        place = jnp.bitwise_xor(info_ref[1], t)
        mine = [c for r, c in enumerate(chunks) if quad_of(r, groups_y) == t]
        total = mine[0][...].astype(jnp.float32)
        for ref in mine[1:]:
            total = total + ref[...].astype(jnp.float32)
        mixed, tail = total[2 * rows : 3 * rows], total[3 * rows :]
        tail = jnp.concatenate([tail[:, k * left : (k + 1) * left] for k in range(parts)], 0)
        zeros = jnp.zeros((rows, room), jnp.float32)
        held[place, 0] = total[:rows]
        held[place, 1] = jnp.concatenate([mixed[:, :over], zeros], 1)
        held[place, 2] = total[rows : 2 * rows]
        held[place, 3] = jnp.concatenate([mixed[:, over:], tail, zeros], 1)
    tiles = outs[0].shape[0] - 2
    for j in range(2):
        values = jnp.concatenate([held[g, j] for g in range(4)], 1) * scale_ref[j : j + 1]
        high, low = (
            jnp.dot(v, regroup_ref[...], preferred_element_type=jnp.float32).astype(jnp.bfloat16)
            for v in split_rows(values)
        )
        for k in range(4):
            if j * 4 + k < tiles:
                low_ref[j * 4 + k] = low[:, k * LANES : (k + 1) * LANES]
                for out in outs:
                    out[j * 4 + k] = high[:, k * LANES : (k + 1) * LANES]
    for r, out in enumerate(outs):
        for j in range(2):
            value = held[jnp.bitwise_xor(info_ref[4], r), 2 + j] * scale
            out[tiles + j] = value.astype(jnp.bfloat16)
    mode_gradients(*consts, outs[0], low_ref, mode_ref)


def packed_rows(tiles, rows, used):
    top = -(-rows // 16) * 8 if 2 * used <= LANES else rows
    return top, (tiles - 1) * rows + top


def split_rows(values):
    high = values.astype(jnp.bfloat16)
    return high, (values - high.astype(jnp.float32)).astype(jnp.bfloat16)


def mode_gradients(spread_ref, gather_ref, w_ref, s_ref, low_ref, out_ref):
    tiles, rows = s_ref.shape[0] - 2, s_ref.shape[1]
    last, _, _, width = w_ref.shape
    half = spread_ref.shape[1] // (2 * LANES)
    twice = jnp.concatenate([spread_ref[...], spread_ref[...]], 0)
    for tile in range(tiles):
        values = jnp.concatenate([s_ref[tile], low_ref[tile]], 1)
        wide = jnp.dot(values, twice, preferred_element_type=jnp.float32)
        products = []
        for h in range(half):
            kz = tile * half + h
            if kz >= last:
                continue
            out_re = wide[:, (2 * h) * LANES : (2 * h + 1) * LANES]
            out_im = wide[:, (2 * h + 1) * LANES : (2 * h + 2) * LANES]
            real, imag = [], []
            for k in range(width // LANES):
                lane = slice(k * LANES, (k + 1) * LANES)
                w_re = w_ref[kz, 0, :, lane].astype(jnp.float32)
                w_im = w_ref[kz, 1, :, lane].astype(jnp.float32)
                real.append(w_re * out_re + w_im * out_im)
                imag.append(w_re * out_im - w_im * out_re)
            products += [jnp.concatenate(real, 1), jnp.concatenate(imag, 1)]
        high, low = split_rows(jnp.concatenate(products, 0))
        sums = jnp.dot(high, gather_ref[...], preferred_element_type=jnp.float32)
        sums += jnp.dot(low, gather_ref[...], preferred_element_type=jnp.float32)
        which = lax.broadcasted_iota(jnp.int32, (rows, LANES), 1) // (LANES // (2 * half))
        out = sums[:rows]
        for k in range(1, len(products)):
            out = jnp.where(which == k, sums[k * rows : (k + 1) * rows], out)
        out = jnp.where(which < len(products), out, 0.0)
        top = out_ref.shape[0] - (tiles - 1) * rows
        if tile == tiles - 1 and top < rows:
            lower = out[top:]
            if 2 * top > rows:
                zeros = jnp.zeros((2 * top - rows, LANES), jnp.float32)
                lower = jnp.concatenate([lower, zeros], 0)
            out = jnp.concatenate([out[:top, : LANES // 2], lower[:, : LANES // 2]], 1)
        out_ref[tile * rows : tile * rows + out.shape[0]] = out.astype(jnp.bfloat16)


def mix(info, chunks, scale, norm, regroup, spread, gather, weight, sizes):
    tiles, rows, over, scenes, groups_y = sizes
    half = spread.shape[1] // (2 * LANES)
    used = (MZ - (tiles - 1) * half) * spread.shape[0] // half
    out = jax.ShapeDtypeStruct((tiles + 2, rows, LANES), jnp.bfloat16)
    modes = jax.ShapeDtypeStruct((packed_rows(tiles, rows, used)[1], LANES), jnp.bfloat16)
    results = pl.pallas_call(
        functools.partial(mix_kernel, len(chunks), groups_y, over, norm),
        out_shape=[modes] + [out] * scenes,
        in_specs=[IN_SMEM] + [IN_VMEM] * (5 + len(chunks)),
        out_specs=[IN_VMEM] * (1 + scenes),
        scratch_shapes=[
            pltpu.VMEM((4, 4, rows, LANES), jnp.float32),
            pltpu.VMEM((tiles, rows, LANES), jnp.bfloat16),
        ],
        compiler_params=params(24),
        cost_estimate=pl.CostEstimate(
            flops=8 * tiles * rows * gather.size, bytes_accessed=2 * weight.size, transcendentals=0
        ),
        name="mix",
    )(info, *resident(scale, regroup, spread, gather, weight), *chunks)
    return results[0], results[1:]


def outer_kernel(scenes, spread_ref, pick_ref, *refs):
    spectra, out_ref = refs[:scenes], refs[scenes]
    rows = spectra[0].shape[1]
    copies = pick_ref.shape[2] // (2 * LANES)
    last = out_ref.shape[0] // (2 * copies * rows)
    wide = copies * LANES
    half = spread_ref.shape[1] // (2 * LANES)
    per_tile = pick_ref.shape[0]
    tiles = spectra[0].shape[0] - 2
    for kz in range(last):
        if kz % half == 0:
            grads = jnp.dot(
                jnp.concatenate([ref[kz // half] for ref in spectra], 0),
                spread_ref[...],
                preferred_element_type=jnp.float32,
            )
        if kz % per_tile == 0:
            field = jnp.concatenate([ref[tiles + kz // per_tile] for ref in spectra], 0)
        hats = jnp.dot(field, pick_ref[kz % per_tile], preferred_element_type=jnp.float32)
        lane = 2 * (kz % half) * LANES
        for k in range(wide // LANES):
            real, imag = 0.0, 0.0
            for s in range(scenes):
                here = slice(s * rows, (s + 1) * rows)
                hat_re = hats[here, k * LANES : (k + 1) * LANES]
                hat_im = hats[here, wide + k * LANES : wide + (k + 1) * LANES]
                out_re = grads[here, lane : lane + LANES]
                out_im = grads[here, lane + LANES : lane + 2 * LANES]
                real += out_re * hat_re + out_im * hat_im
                imag += out_im * hat_re - out_re * hat_im
            for part, value in enumerate((real, imag)):
                first = (kz * copies + k) * 2 + part
                out_ref[pl.ds(first, rows, stride=2 * copies * last), :] = value


def outer(spectra, spread, pick):
    tiles, rows, _ = spectra[0].shape
    wide = pick.shape[2] // 2
    return pl.pallas_call(
        functools.partial(outer_kernel, len(spectra)),
        out_shape=jax.ShapeDtypeStruct((rows * MZ * wide // LANES * 2, LANES), jnp.float32),
        in_specs=[IN_VMEM] * (2 + len(spectra)),
        out_specs=IN_VMEM,
        compiler_params=params(16),
        cost_estimate=pl.CostEstimate(
            flops=2 * tiles * rows * 4 * LANES * 12 * LANES,
            bytes_accessed=16 * tiles * rows * wide + 8 * tiles * rows * LANES * len(spectra),
            transcendentals=0,
        ),
        name="outer",
    )(*resident(spread, pick), *spectra)


def local_kernel(row_ref, column_ref, point_ref, grad_ref, out_ref, mixing):
    channels, cells_x, cells_y, length = grad_ref.shape
    picked = lax.dot_general(row_ref[...], point_ref[...], NT, preferred_element_type=jnp.float32)
    spread = jnp.dot(
        picked.astype(jnp.bfloat16), column_ref[...], preferred_element_type=jnp.float32
    )
    row = lax.broadcasted_iota(jnp.int32, spread.shape, 0) % cells_y
    column = lax.broadcasted_iota(jnp.int32, spread.shape, 1) % cells_y
    mixing[...] = jnp.where(row == column, spread, 0.0).astype(jnp.bfloat16)

    @pl.loop(0, cells_x, step=4)
    def _(start):
        for x in range(4):
            out_ref[start + x] = jnp.dot(
                mixing[...],
                grad_ref[:, start + x].reshape(channels * cells_y, length),
                preferred_element_type=jnp.float32,
            ).astype(out_ref.dtype)


def local(cell_rows, cell_columns, point, grad):
    channels, cells_x, cells_y, length = grad.shape
    width = channels * cells_y
    return pl.pallas_call(
        local_kernel,
        out_shape=jax.ShapeDtypeStruct((cells_x, width, length), jnp.bfloat16),
        in_specs=[IN_VMEM] * 4,
        out_specs=IN_VMEM,
        scratch_shapes=[pltpu.VMEM((width, width), jnp.bfloat16)],
        compiler_params=params(16),
        cost_estimate=pl.CostEstimate(
            flops=2 * grad.size * width, bytes_accessed=4 * grad.size, transcendentals=0
        ),
        name="local",
    )(*resident(cell_rows, cell_columns, point, grad))


def inverse_kernel(groups, per_tile, here, info_ref, t_ref, order_ref, z_ref, local_ref, *refs):
    chunks, (out_ref, modes, held, built, sems) = refs[:groups], refs[groups:]
    channels, cells_x, cells_y, length = built.shape
    rows = modes.shape[0] // groups
    tiles = channels // per_tile
    last = modes.shape[1] // LANES - 1
    top = chunks[0].shape[0] - last * rows
    for r in range(groups):
        own = pl.ds(pl.multiple_of(jnp.bitwise_xor(info_ref[0], r) * rows, 8), rows)
        for j in range(last):
            value = chunks[r][j * rows : (j + 1) * rows]
            modes[own, j * LANES : (j + 1) * LANES] = value.astype(jnp.float32)
        value = chunks[r][last * rows :].astype(jnp.float32)
        if top < rows:
            middle = LANES // 2
            value = jnp.concatenate([value[:, :middle], value[: rows - top, middle:]], 0)
            value = jnp.concatenate([value, jnp.zeros_like(value)], 1)
        modes[own, last * LANES :] = value
    gathered = modes[...].astype(jnp.bfloat16)
    gathered = jnp.concatenate([gathered, gathered], 0)
    sums = jnp.dot(t_ref[info_ref[3]], gathered, preferred_element_type=jnp.float32)
    cells = sums.shape[0] // 2
    cosine, sine = sums[:cells], sums[cells:]
    wide = sine.shape[1]
    lane = lax.broadcasted_iota(jnp.int32, sine.shape, 1)
    first = lane % (2 * channels) < channels
    turned = jnp.where(
        first, -pltpu.roll(sine, wide - channels, 1), pltpu.roll(sine, channels, 1)
    )
    back = (cosine + turned).astype(jnp.bfloat16)
    ordered = jnp.dot(back, order_ref[...], preferred_element_type=jnp.float32)
    held[...] = ordered.astype(jnp.bfloat16).reshape(held.shape)

    span = tiles * cells_y
    copies = []
    for start in range(0, cells_x, here):
        stack = []
        for x in range(start, start + here):
            back = held[x]
            stack += [back[:, k * LANES : (k + 1) * LANES] for k in range(tiles)]
        stack = jnp.concatenate(stack, 0)
        spectral = jnp.dot(
            jnp.concatenate([stack, stack], 1), z_ref[...], preferred_element_type=jnp.float32
        )
        for x in range(here):
            for j in range(per_tile):
                both = (
                    spectral[x * span : (x + 1) * span, j * length : (j + 1) * length]
                    + local_ref[start + x, j * span : (j + 1) * span].astype(jnp.float32)
                ).astype(jnp.bfloat16)
                for k in range(tiles):
                    built[k * per_tile + j, start + x] = both[k * cells_y : (k + 1) * cells_y]
        copies.append(
            pltpu.make_async_copy(
                built.at[:, pl.ds(start, here)],
                out_ref.at[:, pl.ds(start, here)],
                sems.at[start // here],
            )
        )
        copies[-1].start()
    for copy in copies:
        copy.wait()


def inverse(info, chunks, table, order, z_table, local_part, shape, per_tile, here):
    channels, cells_x, cells_y, length = shape
    return pl.pallas_call(
        functools.partial(inverse_kernel, len(chunks), per_tile, here),
        out_shape=jax.ShapeDtypeStruct(shape, jnp.bfloat16),
        in_specs=[IN_SMEM] + [IN_VMEM] * (4 + len(chunks)),
        out_specs=IN_HBM,
        scratch_shapes=[
            pltpu.VMEM((table.shape[2] // 2, order.shape[0]), jnp.float32),
            pltpu.VMEM((cells_x, cells_y, order.shape[1]), jnp.bfloat16),
            pltpu.VMEM(shape, jnp.bfloat16),
            pltpu.SemaphoreType.DMA((cells_x // here,)),
        ],
        compiler_params=params(28),
        cost_estimate=pl.CostEstimate(
            flops=2 * local_part.size * LANES, bytes_accessed=4 * local_part.size, transcendentals=0
        ),
        name="inverse",
    )(info, *resident(table, order, z_table, local_part), *chunks)


def flip(value, axes, size, r):
    return lax.ppermute(value, axes, [(i, i ^ r) for i in range(size)])


def body(field_in, grad_pre, spec_weight, point_weight):
    _, channels, cells_x, cells_y, cells_z = field_in.shape
    groups_x, groups_y = lax.axis_size("gx"), lax.axis_size("gy")
    groups, scenes = groups_x * groups_y, lax.axis_size("scene")
    group_axes = ("gx", "gy")
    total_x, total_y = cells_x * groups_x, cells_y * groups_y
    cells = cells_x * cells_y
    norm = float(total_x * total_y * cells_z) ** -0.5
    modes_xd, modes_yd = spec_weight.shape[:2]
    modes = modes_xd * modes_yd
    rows = -(-modes // 8) * 8
    half = LANES // (2 * channels)
    tiles = -(-MZ // half)
    block = channels // 4
    slot = 16
    per_tile = LANES // (2 * slot)
    sizes = (groups, groups_y, modes_xd, modes_yd, total_x, total_y)

    me = lax.axis_index(group_axes)
    at_x, at_y = lax.axis_index("gx"), lax.axis_index("gy")
    quad = at_x % 2 * 2 + at_y % 2
    base, turns = (jnp.asarray(t) for t in forward_table(rows, sizes, cells_x, cells_y))
    if groups * groups * rows * 2 * cells <= 1 << 24:
        inverse_t = jnp.asarray(
            np.stack([inverse_table(np, i, rows, sizes, cells_x, cells_y) for i in range(groups)])
        )
        inverse_at = me
    else:
        inverse_t = inverse_table(jnp, me, rows, sizes, cells_x, cells_y)[None]
        inverse_at = 0 * me
    forward_at = at_x // 2 * (groups_y // 2) + at_y // 2
    info = jnp.stack([me, quad, forward_at, inverse_at, lax.axis_index("scene")])

    regroup = jnp.asarray(regroup_table(channels, block, half))
    inverse_z = jnp.asarray(inverse_z_table(cells_z, per_tile, slot, norm))
    order = jnp.asarray(order_table(channels, tiles * half, per_tile, slot))
    lane = np.arange(LANES)
    spread = jnp.asarray(spread_table(channels, half, lane % channels))
    gather = jnp.asarray(gather_table(channels, LANES // channels))
    here = channels // scenes
    pair = np.arange(here * channels)
    kz_tile = LANES // (2 * block)
    pick = spread_table(here, kz_tile, pair // channels).reshape(LANES, kz_tile, -1)
    pick = jnp.asarray(pick.transpose(1, 0, 2))
    cell_rows, cell_columns = (jnp.asarray(t) for t in cell_tables(channels, per_tile, cells_y))
    scale = np.full((2, 4, kz_tile, 2 * block), 2.0 * norm, np.float32)
    scale[0, :, 0] = norm
    scale = jnp.asarray(scale.reshape(2, 4 * LANES))

    def cells_of(field):
        mine = along_z(info, field.reshape(channels, cells, cells_z), block)
        return [mine[0]] + [
            flip(mine[t], group_axes, groups, quad_offset(t, groups_y)) for t in range(1, 4)
        ]

    grad_cells = cells_of(grad_pre)
    field, _ = lax.optimization_barrier((field_in, grad_cells[0]))
    field_cells = cells_of(field)
    grad_sums, table = first_plane(info, grad_cells, base, turns, block)
    sums = second_plane(info, field_cells, table, grad_sums, groups, rows, block)
    got = {0: sums[0], 1: flip(sums[1], group_axes, groups, 1)}
    far = [r for r in range(groups - 1, 1, -1) if r % groups_y >= groups_y // 2]
    for r in far:
        got[r] = flip(sums[r], group_axes, groups, r)
    near = [r for r in range(2, groups) if r not in far]
    waiting, _ = lax.optimization_barrier(([sums[r] for r in near], got[1]))
    for r, value in zip(near, waiting):
        got[r] = flip(value, group_axes, groups, r)
    got = [got[r] for r in range(groups)]
    weight = spec_weight.reshape(modes, MZ, 2, channels * channels)
    weight = jnp.pad(weight.transpose(1, 2, 0, 3), ((0, 0), (0, 0), (0, rows - modes), (0, 0)))
    local_part = local(
        cell_rows,
        cell_columns,
        point_weight,
        grad_pre.reshape(channels, cells_x, cells_y, cells_z),
    )
    got, weight, local_part = lax.optimization_barrier((got, weight, local_part))
    over = 2 * MZ * block - LANES
    mode_grad, spectra = mix(
        info,
        got,
        scale,
        norm,
        regroup,
        spread,
        gather,
        weight,
        (tiles, rows, over, scenes, groups_y),
    )

    along_y = [mode_grad] + [None] * (groups_y - 1)
    for r in range(groups_y - 1, 0, -1):
        along_y[r] = flip(mode_grad, "gy", groups_y, r)
    gathered = list(along_y)
    for r in range(1, groups_x):
        for k, value in enumerate(along_y):
            if k == 1:
                gathered.append(flip(mode_grad, group_axes, groups, r * groups_y + k))
            else:
                gathered.append(flip(value, "gx", groups_x, r))

    got = [spectra[0]]
    for r in range(1, scenes):
        after = mode_grad if r == 2 else along_y[1] if r == 3 else along_y[-1]
        value, _ = lax.optimization_barrier((spectra[r], after))
        got.append(flip(value, "scene", scenes, r))
    spectra = got
    grad_field = inverse(
        info,
        gathered,
        inverse_t,
        order,
        inverse_z,
        local_part,
        (channels, cells_x, cells_y, cells_z),
        per_tile,
        2,
    )
    spectra, grad_field = lax.optimization_barrier((spectra, grad_field))
    grads = outer(spectra, spread, pick)
    grads = grads.reshape(rows, MZ, here * channels // LANES, 2, LANES)[:modes]
    grad_spec = grads.transpose(0, 1, 3, 2, 4).reshape(
        modes_xd, modes_yd, MZ, 2, here * channels
    )

    return grad_field[None], grad_spec


def solution(mesh):
    return jax.shard_map(
        body,
        mesh=mesh,
        in_specs=(
            P("scene", None, "gx", "gy", None),
            P("scene", None, "gx", "gy", None),
            P("gx", "gy", None, None, None),
            P(),
        ),
        out_specs=(P("scene", None, "gx", "gy", None), P("gx", "gy", None, None, "scene")),
        check_vma=False,
    )
```
